256 devices in a mesh: grp: 16 (over x, y_hi, core), shard: 16 (over z, y_lo).
Axes of the slice: x: 4, y: 4 (y_hi: 2, y_lo: 2; y = y_hi * 2 + y_lo), z: 8, core: 2. Of those that a mesh axis runs over, the one named last changes fastest.
Arguments:
- entities: float32 [262144, 256], P(('grp', 'shard')), may hold values from -1.5 to 1.5
- row_acc: float32 [262144], P(('grp', 'shard')), may hold values from 0.01 to 0.1
- relations: float32 [4096, 256], replicated, may hold values from 0.1 to 1.9
- rel_acc: float32 [4096], replicated, may hold values from 0.0005 to 0.01
- src_row: int32 [2, 16, 16, 1152], P(None, 'grp', 'shard'), may hold values from 0 to 1023
- rel_id: int32 [2, 16, 16, 1152], P(None, 'grp', 'shard'), may hold values from 0 to 4095
- dst_owner: int32 [2, 16, 16, 1152, 1], P(None, 'grp', 'shard'), may hold values from 0 to 15; in each aligned block of 1152 rows (0 to 1151, 1152 to 2303, ..., all dimensions but the last counted through in order) at most 144 rows name the same one
- dst_row: int32 [2, 16, 16, 1152], P(None, 'grp', 'shard'), may hold values from 0 to 1023
- neg_rows: int32 [2, 16, 1024], P(None, 'grp', 'shard'), may hold values from 0 to 1023
- lengths: int32 [2, 16, 16], P(None, 'grp', 'shard'), may hold values from 1 to 1152, 6144 in all within a row
Outputs:
- new_entities: float32 [262144, 256], P(('grp', 'shard'))
- new_row_acc: float32 [262144], P(('grp', 'shard'))
- new_relations: float32 [4096, 256], replicated
- new_rel_acc: float32 [4096], replicated
The draws below stay inside these ranges and needn't reach their ends.
Inputs may be any that keep to these rules, and one draw needn't show every extreme that they name: `dst_owner`: at most 144 of one device's 1152 edge slots name one shard index; some device reaches it. In each round a group's 16 lengths sum to 6144 and the largest is 1152; a device's live edges are its first slots. `src_row`: the edge slots of device (g, s) have sources among that device's own rows.
All inputs are finite; a program needn't handle non-finite values.
Results may differ from the reference program's by a relative error of at most 0.0045.
Values may be sent and summed in bfloat16 or wider, within the bound.
A program may use at most 128 MiB of HBM per device.

```python
import math
import jax
import jax.numpy as jnp
import numpy as np
from jax import lax

D = 256
RELS = 4096
NNEG = 1024
ROWS_DEV = 1024
MEAN = 384
EDGES_DEV = 1152
CAP = 144
ENTITIES = 262144
N_GRP = 16
N_SHARD = 16


def place_ends(drawn, key, low, top_value):
    longest = drawn.shape.index(max(drawn.shape))
    spots = []
    for shift in (0, 1):
        where = [jax.random.randint(jax.random.fold_in(key, axis), (), 0, length) for axis, length in enumerate(drawn.shape)]
        where[longest] = (where[longest] + shift) % drawn.shape[longest]
        spots.append(tuple(where))
    return drawn.at[spots[0]].set(low).at[spots[1]].set(top_value)


def shard_levels(stream_key, shape, cuts, low, high):
    loudness = 1.0
    for position, blocks in cuts:
        heights = jax.random.uniform(jax.random.fold_in(jax.random.fold_in(stream_key, 6), position), (blocks,), jnp.float32, low / len(cuts), high / len(cuts))
        loudness = loudness * jnp.repeat(jnp.exp(heights), shape[position] // blocks).reshape((-1,) + (1,) * (len(shape) - 1 - position))
    return loudness


def rank_table(count, lean):
    weights = [(1 << 20) // math.isqrt(grade ** lean) + 1 for grade in range(1, count + 1)]
    scale = 1 + sum(weights) // (1 << 30)
    return np.cumsum(np.array([max(1, weight // scale) for weight in weights]))


def ranked_ids(rng, dims, number_of, slope):
    listing = rank_table(number_of, slope)
    ticket = jax.random.randint(jax.random.fold_in(rng, 1), dims, 0, int(listing[number_of - 1]))
    grade = jnp.searchsorted(jnp.asarray(listing, jnp.int32), ticket, side="right")
    return jax.random.permutation(jax.random.fold_in(rng, 2), number_of)[grade].astype(jnp.int32)


def split_up(amount, total, most, lean):
    portions = [(1 << 20) // math.isqrt(rank ** lean) + 1 for rank in range(2, amount + 1)]
    surplus, given = total - most - (amount - 1), [1] * (amount - 1)
    while surplus > 0:
        free = [i for i in range(amount - 1) if given[i] < most]
        pool, left = sum([portions[i] for i in free]), surplus
        for i in free:
            more = min(most - given[i], max(1, left * portions[i] // pool), surplus)
            given[i] = given[i] + more
            surplus = surplus - more
    return np.array([most] + given)


def uneven_parts(stream_key, amount, total, bound, slope):
    if amount == 2:
        one = jax.random.randint(stream_key, (), max(1, total - bound), min(bound, total - 1) + 1)
        return jnp.stack([one, total - one])
    sizes = jnp.asarray(split_up(amount, total, bound, slope), jnp.int32)
    twos = (amount - 1) // 2
    source_of, sink = sizes[1:1 + 2 * twos:2], sizes[2:2 + 2 * twos:2]
    margin = jnp.minimum(source_of - 1, bound - sink)
    passed = jax.random.randint(jax.random.fold_in(stream_key, 1), (twos,), 0, 1 << 20) % (margin + 1)
    sizes = sizes.at[1:1 + 2 * twos:2].set(source_of - passed).at[2:2 + 2 * twos:2].set(sink + passed)
    return sizes[jax.random.permutation(jax.random.fold_in(stream_key, 2), amount)]


def deal_out(own_key, own, number, rows, number_of, top, most, lean):
    order = jax.random.permutation(own_key, number_of)
    crowded, common = load_shares(number_of, rows * top, most, lean, True), load_shares(number_of, rows * top, most, lean, False)
    places = jnp.arange(number_of)

    def named(sizes, offset_by):
        used = int((sizes > 0).sum())
        fixed = max(1, used // 4)
        shifted = fixed + (places - fixed + offset_by * (used - fixed)) % max(1, number_of - fixed)
        return jnp.zeros((number_of,), jnp.int32).at[order[jnp.where(places < fixed, places, shifted)]].set(jnp.asarray(sizes, jnp.int32))

    sizes = jnp.where(number % 4 == 0, named(crowded, number // 4), named(common, number - number // 4 - 1))
    mixed = jax.random.permutation(jax.random.fold_in(own, 3), number_of)
    donor, receiver = mixed[0:number_of // 2 * 2:2], mixed[1:number_of // 2 * 2:2]
    room = jnp.minimum(sizes[donor] - 1, most - sizes[receiver]) // 2
    room = jnp.where((donor == order[0]) | (receiver == order[0]) | (sizes[receiver] == 0), 0, jnp.maximum(room, 0))
    shifted = jax.random.randint(jax.random.fold_in(own, 4), (number_of // 2,), 0, 1 << 20) % (room + 1)
    sizes = sizes.at[donor].add(-shifted).at[receiver].add(shifted)
    labels = jnp.searchsorted(jnp.cumsum(sizes), jnp.arange(rows * top), side="right").astype(jnp.int32)
    listing = labels.reshape(top, rows).T
    listing = listing[jax.random.permutation(jax.random.fold_in(own, 1), rows)]
    offset_by = jax.random.randint(jax.random.fold_in(own, 2), (rows, 1), 0, top)
    return jnp.take_along_axis(listing, (jnp.arange(top)[None, :] + offset_by) % top, axis=1)


def load_shares(number_of, total, limit, slope, full):
    portions = [(1 << 20) // math.isqrt(standing ** slope) + 1 for standing in range(1, number_of + 1)]
    largest = limit if full else min(limit, max(-(-total // number_of), total * portions[0] // sum(portions)))
    least = 1 if total - largest >= number_of - 1 else 0
    given, surplus = [largest] + [least] * (number_of - 1), total - largest - least * (number_of - 1)
    while surplus > 0:
        free = [i for i in range(1, number_of) if given[i] < largest] or [i for i in range(1, number_of) if given[i] < limit]
        pool, remaining = sum([portions[i] for i in free]), surplus
        for i in free:
            more = min(limit - given[i], max(1, remaining * portions[i] // pool), surplus)
            given[i] = given[i] + more
            surplus = surplus - more
    return np.array(given)


def noise(stream_key, shape, scale, reach, cuts=(), kind=jnp.bfloat16):
    factor_of = shard_levels(stream_key, shape, cuts, -0.22, 0.18) if cuts else 1.0
    drawn = jax.random.normal(stream_key, shape, jnp.float32) * scale * factor_of
    return jnp.minimum(jnp.maximum(drawn, -reach), reach).astype(kind)


def setup_inputs(seed: int = 0) -> dict:
    splits = jax.random.split(jax.random.key(seed), 11)
    entities = noise(splits[0], (ENTITIES, D), 0.25, 1.5, ((0, 256),), jnp.float32)
    row_acc = jnp.clip(jnp.exp(math.log(0.1) - 2.3025851 * jax.random.uniform(splits[1], (ENTITIES,), jnp.float32) ** shard_levels(splits[1], (ENTITIES,), ((0, 256),), -0.2, 0.2)), 0.01, 0.1)
    relations = jnp.clip(1.0 + 0.18 * jax.random.normal(splits[2], (RELS, D), jnp.float32), 0.1, 1.9)
    rel_acc = jnp.clip(jnp.exp(jax.random.uniform(splits[3], (RELS,), jnp.float32, math.log(0.0005), math.log(0.01))), 0.0005, 0.01)
    src_row = place_ends(jax.random.randint(splits[4], (2, N_GRP, N_SHARD, EDGES_DEV), 0, ROWS_DEV), jax.random.fold_in(splits[4], 1), 0, ROWS_DEV - 1).astype(jnp.int32)
    rel_id = place_ends(ranked_ids(splits[5], (2, N_GRP, N_SHARD, EDGES_DEV), RELS, 2), jax.random.fold_in(splits[5], 3), 0, RELS - 1).astype(jnp.int32)
    dst_owner_keys = jax.random.split(jax.random.fold_in(splits[6], 1), 2 * N_GRP * N_SHARD * EDGES_DEV // EDGES_DEV)
    dst_owner_turns = jax.random.permutation(jax.random.fold_in(splits[6], 3), 2 * N_GRP * N_SHARD * EDGES_DEV // EDGES_DEV)
    dst_owner = jax.vmap(lambda own, number: deal_out(jax.random.fold_in(splits[6], 2), own, number, EDGES_DEV, N_SHARD, 1, CAP, 1))(dst_owner_keys, dst_owner_turns).reshape((2, N_GRP, N_SHARD, EDGES_DEV, 1))
    dst_row = place_ends(jax.random.randint(splits[7], (2, N_GRP, N_SHARD, EDGES_DEV), 0, ROWS_DEV), jax.random.fold_in(splits[7], 1), 0, ROWS_DEV - 1).astype(jnp.int32)
    neg_rows = place_ends(jax.random.randint(splits[8], (2, N_GRP, NNEG), 0, ROWS_DEV), jax.random.fold_in(splits[8], 1), 0, ROWS_DEV - 1).astype(jnp.int32)
    lengths = jax.vmap(lambda own: uneven_parts(own, N_SHARD, N_SHARD * MEAN, EDGES_DEV, 2))(jax.random.split(splits[9], 2 * N_GRP)).reshape((2, N_GRP, N_SHARD)).astype(jnp.int32)
    return {"entities": entities, "row_acc": row_acc, "relations": relations, "rel_acc": rel_acc, "src_row": src_row, "rel_id": rel_id, "dst_owner": dst_owner, "dst_row": dst_row, "neg_rows": neg_rows, "lengths": lengths}


LEARN_RATE = 0.3

def adagrad(table, accum, gradient):
    total = accum + lax.optimization_barrier(jnp.mean(gradient * gradient, axis=-1))
    return (table - LEARN_RATE * gradient / jnp.sqrt(total)[..., None], total)

def bucket(src_part, dst_part, relations, src_rows, rel_ids, owners, dst_rows, neg_list, live_len):
    shards = src_part.shape[0]
    per_shard = src_part.shape[1]
    width = src_part.shape[2]
    edges = src_rows.shape[-1]
    live = jnp.arange(edges, dtype=jnp.int32)[None, :] < live_len[:, None]
    picked = jnp.nonzero(live.reshape(-1), size=shards * MEAN)[0].astype(jnp.int32)
    shard_of = picked // edges
    src_index = shard_of * per_shard + src_rows.reshape(-1)[picked]
    dst_index = owners.reshape(-1)[picked] * per_shard + dst_rows.reshape(-1)[picked]
    rel_index = rel_ids.reshape(-1)[picked]
    neg_index = jnp.arange(NNEG, dtype=jnp.int32) // (NNEG // shards) * per_shard + neg_list
    src_flat = src_part.reshape(-1, width)
    dst_flat = dst_part.reshape(-1, width)
    src_emb = src_flat[src_index].astype(jnp.bfloat16)
    dst_emb = dst_flat[dst_index]
    negatives = dst_flat[neg_index]
    rel_rows = relations[rel_index]
    query = src_emb.astype(jnp.float32) * rel_rows
    query_bf = query.astype(jnp.bfloat16)
    positive = lax.optimization_barrier(jnp.sum(query * dst_emb.astype(jnp.float32), axis=-1))
    negative_sc = jnp.dot(query_bf, negatives.T, preferred_element_type=jnp.float32)
    pos_weight = -jax.nn.sigmoid(-positive)
    neg_weight = (jax.nn.sigmoid(negative_sc) / NNEG).astype(jnp.bfloat16)
    query_grad = pos_weight[:, None] * dst_emb.astype(jnp.float32) + jnp.dot(neg_weight, negatives, preferred_element_type=jnp.float32)
    src_grad = query_grad * rel_rows
    rel_grad_rows = query_grad * src_emb.astype(jnp.float32)
    dst_grad = pos_weight[:, None] * query
    neg_grad = jnp.dot(neg_weight.T, query_bf, preferred_element_type=jnp.float32)
    zero_rows = jnp.zeros((shards * per_shard, width), jnp.float32)
    src_total = zero_rows.at[src_index].add(src_grad).reshape(shards, per_shard, width)
    dst_total = zero_rows.at[dst_index].add(dst_grad).at[neg_index].add(neg_grad).reshape(shards, per_shard, width)
    rel_total = jax.ops.segment_sum(rel_grad_rows, rel_index, num_segments=relations.shape[0])
    return (src_total, dst_total, rel_total)

def reference(entities, row_acc, relations, rel_acc, src_row, rel_id, dst_owner, dst_row, neg_rows, lengths):
    table = entities.reshape(N_GRP, N_SHARD, ROWS_DEV, D)
    accum = row_acc.reshape(N_GRP, N_SHARD, ROWS_DEV)

    def one_round(src_tables, dst_tables, turn):

        def per_group(pieces):
            return bucket(pieces[0], pieces[1], relations, pieces[2], pieces[3], pieces[4], pieces[5], pieces[6], pieces[7])
        return lax.map(per_group, (src_tables, dst_tables, src_row[turn], rel_id[turn], dst_owner[turn], dst_row[turn], neg_rows[turn], lengths[turn]))
    first_src, first_dst, first_rel = one_round(table, table.astype(jnp.bfloat16), 0)
    table_one, accum_one = adagrad(table, accum, first_src + first_dst)
    partner = jnp.roll(table_one, -1, axis=0).astype(jnp.bfloat16)
    second_src, second_dst, second_rel = one_round(table_one, partner, 1)
    table_two, accum_two = adagrad(table_one, accum_one, second_src + jnp.roll(second_dst, 1, axis=0))
    rel_total = lax.optimization_barrier(jnp.sum(first_rel, axis=0)) + lax.optimization_barrier(jnp.sum(second_rel, axis=0))
    new_rel, new_racc = adagrad(relations, rel_acc, rel_total)
    return (table_two.reshape(-1, D), accum_two.reshape(-1), new_rel, new_racc)
```

```python
import functools
import jax
import jax.numpy as jnp
from jax import lax
from jax.experimental import pallas as pl
from jax.experimental.pallas import tpu as pltpu
from jax.sharding import PartitionSpec as P

LEARN_RATE = 0.3
MESH = pl.DeviceIdType.MESH
F32 = jnp.float32
BF16 = jnp.bfloat16


def adagrad(table, accum, gradient):
    total = accum + jnp.mean(gradient * gradient, axis=-1)
    return (table - LEARN_RATE * gradient / jnp.sqrt(total)[..., None], total)


def exchange_kernel(shifts, groups, shards, *refs):
    count = len(shifts)
    ins, outs = refs[:count], refs[count : 2 * count]
    send_sem, recv_sem, own_sem = refs[2 * count :]
    g, s = lax.axis_index("grp"), lax.axis_index("shard")
    barrier = pltpu.get_barrier_semaphore()
    total = 0
    for shift in shifts:
        source_group = lax.rem(g + groups - shift, groups)
        for k in range(0 if shift else 1, shards):
            source = lax.rem(s + shards - k, shards)
            pl.semaphore_signal(
                barrier, inc=1, device_id=(source_group, source), device_id_type=MESH
            )
            total += 1
    pl.semaphore_wait(barrier, total)
    copies = []
    for a, shift in enumerate(shifts):
        for k in list(range(1, shards)) + [0]:
            target = lax.rem(s + k, shards)
            if shift == 0 and k == 0:
                copy = pltpu.make_async_copy(ins[a].at[s], outs[a].at[s], own_sem.at[a])
            else:
                copy = pltpu.make_async_remote_copy(
                    src_ref=ins[a].at[target],
                    dst_ref=outs[a].at[s],
                    send_sem=send_sem.at[a * shards + k],
                    recv_sem=recv_sem.at[a * shards + k],
                    device_id=(lax.rem(g + groups + shift, groups), target),
                    device_id_type=MESH,
                )
            copy.start()
            copies.append(copy)
    for copy in copies:
        copy.wait()


def exchange(arrays, shifts, collective_id):
    groups, shards = lax.axis_size("grp"), lax.axis_size("shard")
    count = len(arrays)
    return pl.pallas_call(
        functools.partial(exchange_kernel, shifts, groups, shards),
        out_shape=[jax.ShapeDtypeStruct(a.shape, a.dtype) for a in arrays],
        in_specs=[pl.BlockSpec(memory_space=pl.ANY)] * count,
        out_specs=[pl.BlockSpec(memory_space=pl.ANY)] * count,
        scratch_shapes=[
            pltpu.SemaphoreType.DMA((count * shards,)),
            pltpu.SemaphoreType.DMA((count * shards,)),
            pltpu.SemaphoreType.DMA((count,)),
        ],
        compiler_params=pltpu.CompilerParams(collective_id=collective_id, has_side_effects=True),
        name="exchange",
    )(*arrays)


def relation_kernel(rows, part, whole, got_c, got_x, got_y, got_z, sum_c, sum_x, sum_y, send, recv):
    g, s = lax.axis_index("grp"), lax.axis_index("shard")
    x, y_hi, core = g // 4, lax.rem(g // 2, 2), lax.rem(g, 2)
    z, y_lo = s // 2, lax.rem(s, 2)
    y = y_hi * 2 + y_lo

    def device(x, y, z, core):
        return (x * 4 + (y // 2) * 2 + core, z * 2 + lax.rem(y, 2))

    stages = (
        [(1, lambda k: device(x, y, z, 1 - core), lambda k: 1 - core)]
        + [(3, lambda k: device(lax.rem(x + k, 4), y, z, core), lambda k: lax.rem(x + k, 4))]
        + [(3, lambda k: device(x, lax.rem(y + k, 4), z, core), lambda k: lax.rem(y + k, 4))]
        + [(7, lambda k: device(x, y, lax.rem(z + k, 8), core), lambda k: lax.rem(z + k, 8))]
    )
    firsts = (0, 1, 4, 7)
    barrier = pltpu.get_barrier_semaphore()
    for peers, who, _ in stages:
        for k in range(1, peers + 1):
            pl.semaphore_signal(barrier, inc=1, device_id=who(k), device_id_type=MESH)
    pl.semaphore_wait(barrier, 14)

    sources = (part, sum_c, sum_x, sum_y)
    landings = (got_c, got_x, got_y, got_z)
    own = (core, x, y, z)
    size = rows
    base = 0
    bases = []
    sizes = []
    for stage, (peers, who, place) in enumerate(stages):
        size = size // (peers + 1)
        sizes.append(size)
        src, land = sources[stage], landings[stage]
        copies = []
        for k in range(1, peers + 1):
            copy = pltpu.make_async_remote_copy(
                src_ref=src.at[pl.ds(place(k) * size, size)],
                dst_ref=land.at[k - 1],
                send_sem=send.at[firsts[stage] + k - 1],
                recv_sem=recv.at[firsts[stage] + k - 1],
                device_id=who(k),
                device_id_type=MESH,
            )
            copy.start()
            copies.append(copy)
        for copy in copies:
            copy.wait()
        base = base + own[stage] * size
        bases.append(base)
        tile = min(size, 128)

        def add(i, carry, src=src, land=land, peers=peers, size=size, stage=stage, tile=tile, base=base):
            total = src[pl.ds(own[stage] * size + i * tile, tile), :].astype(F32)
            for k in range(peers):
                total += land[k, pl.ds(i * tile, tile), :].astype(F32)
            if stage < 3:
                sources[stage + 1][pl.ds(i * tile, tile), :] = total.astype(BF16)
            else:
                whole[pl.ds(base + i * tile, tile), :] = total.astype(BF16)
            return carry

        lax.fori_loop(0, size // tile, add, 0)
    for stage in (3, 2, 1, 0):
        peers, who, _ = stages[stage]
        copies = []
        for k in range(1, peers + 1):
            block = whole.at[pl.ds(bases[stage], sizes[stage])]
            copy = pltpu.make_async_remote_copy(
                src_ref=block,
                dst_ref=block,
                send_sem=send.at[14 + firsts[stage] + k - 1],
                recv_sem=recv.at[14 + firsts[stage] + k - 1],
                device_id=who(k),
                device_id_type=MESH,
            )
            copy.start()
            copies.append(copy)
        for copy in copies:
            copy.wait()


def sum_relations(part, collective_id):
    rows, width = part.shape
    vmem = lambda *shape: pltpu.VMEM(shape + (width,), BF16)
    return pl.pallas_call(
        functools.partial(relation_kernel, rows),
        out_shape=jax.ShapeDtypeStruct(part.shape, BF16),
        in_specs=[pl.BlockSpec(memory_space=pltpu.VMEM)],
        out_specs=pl.BlockSpec(memory_space=pltpu.VMEM),
        scratch_shapes=[
            vmem(1, rows // 2),
            vmem(3, rows // 8),
            vmem(3, rows // 32),
            vmem(7, rows // 256),
            vmem(rows // 2),
            vmem(rows // 8),
            vmem(rows // 32),
            pltpu.SemaphoreType.DMA((28,)),
            pltpu.SemaphoreType.DMA((28,)),
        ],
        compiler_params=pltpu.CompilerParams(
            collective_id=collective_id, has_side_effects=True, vmem_limit_bytes=24 << 20
        ),
        name="relation_sum",
    )(part)


def one_hot(index, size):
    return (index[:, None] == jnp.arange(size, dtype=jnp.int32)[None, :]).astype(BF16)


def one_hot_t(index, size):
    return (jnp.arange(size, dtype=jnp.int32)[:, None] == index[None, :]).astype(BF16)


def dot(a, b):
    return jnp.dot(a, b, preferred_element_type=F32)


def plan(owners, dst_rows, shards, capacity, lanes):
    edges = owners.shape[0]
    position = jnp.arange(edges, dtype=jnp.int32)
    chosen = one_hot(owners, shards)
    before = (position[None, :] < position[:, None]).astype(BF16)
    ranks = jnp.sum(dot(before, chosen) * chosen.astype(F32), axis=1).astype(jnp.int32)
    chosen_t = one_hot_t(owners, shards)
    by_rank = one_hot(ranks, lanes)
    high = dot(chosen_t * (dst_rows // 32).astype(BF16)[None, :], by_rank)
    low = dot(chosen_t * (dst_rows % 32).astype(BF16)[None, :], by_rank)
    return owners * capacity + ranks, (high * 32 + low).astype(jnp.int32)


def bucket(table_bf, rel_rows, src_rows, slots, asked, neg_local, live_len, shift, cids):
    shards, capacity = asked.shape
    rows, width = table_bf.shape
    edges = src_rows.shape[0]
    live = jnp.arange(edges, dtype=jnp.int32) < live_len
    negs = neg_local.shape[0]
    wanted = jnp.concatenate(
        [asked, jnp.broadcast_to(neg_local[None, :], (shards, negs))], axis=1
    ).reshape(-1)
    sent = dot(one_hot(wanted, rows), table_bf).astype(BF16).reshape(shards, capacity + negs, width)
    (got,) = exchange([sent], [-shift], cids[0])
    fetched = got[:, :capacity].reshape(-1, width)
    negatives = got[:, capacity:].reshape(-1, width)
    src_emb = dot(one_hot(src_rows, rows), table_bf)
    dst_emb = dot(one_hot(slots, shards * capacity), fetched)
    query = src_emb * rel_rows
    query_bf = query.astype(BF16)
    positive = jnp.sum(query * dst_emb, axis=-1)
    scores = lax.dot_general(
        query_bf, negatives, (((1,), (1,)), ((), ())), preferred_element_type=F32
    )
    pos_weight = jnp.where(live, -jax.nn.sigmoid(-positive), 0.0)
    neg_weight = jnp.where(
        live[:, None], jax.nn.sigmoid(scores) / negatives.shape[0], 0.0
    ).astype(BF16)
    query_grad = pos_weight[:, None] * dst_emb + dot(neg_weight, negatives)
    src_grad = (query_grad * rel_rows).astype(BF16)
    rel_grad = (query_grad * src_emb).astype(BF16)
    dst_grad = (pos_weight[:, None] * query).astype(BF16)
    neg_grad = lax.dot_general(
        neg_weight, query_bf, (((0,), (0,)), ((), ())), preferred_element_type=F32
    ).astype(BF16)
    slot_grad = dot(one_hot_t(slots, shards * capacity), dst_grad).astype(BF16)
    outgoing = jnp.concatenate(
        [slot_grad.reshape(shards, capacity, width), neg_grad.reshape(shards, negs, width)], axis=1
    )
    (incoming,) = exchange([outgoing], [shift], cids[1])
    total = dot(one_hot_t(wanted, rows), incoming.reshape(-1, width))
    total = total + dot(one_hot_t(src_rows, rows), src_grad)
    return total, rel_grad


def per_device(
    entities, row_acc, relations, rel_acc, src_row, rel_id, dst_owner, dst_row, neg_rows, lengths
):
    groups, shards = lax.axis_size("grp"), lax.axis_size("shard")
    edges = src_row.shape[-1]
    capacity = 2 * edges // shards
    lanes = -(-capacity // 128) * 128
    slots, requests = [], []
    for turn in range(2):
        slot, request = plan(
            dst_owner[turn, 0, 0, :, 0], dst_row[turn, 0, 0], shards, capacity, lanes
        )
        slots.append(slot)
        requests.append(request.reshape(shards, 1, lanes))
    asked = exchange(requests, [0, 1], 0)
    asked = [a[:, 0, :capacity] for a in asked]
    rel_ids = rel_id[:, 0, 0].reshape(-1)
    rel_rows = jnp.take(relations, rel_ids, axis=0).reshape(2, edges, -1)
    neg_next = lax.ppermute(
        neg_rows[1, 0], "grp", [(i, (i + 1) % groups) for i in range(groups)]
    )
    first, first_rel = bucket(
        entities.astype(BF16), rel_rows[0], src_row[0, 0, 0], slots[0], asked[0],
        neg_rows[0, 0], lengths[0, 0, 0], 0, (1, 2),
    )
    table_one, accum_one = adagrad(entities, row_acc, first)
    second, second_rel = bucket(
        table_one.astype(BF16), rel_rows[1], src_row[1, 0, 0], slots[1], asked[1],
        neg_next, lengths[1, 0, 0], 1, (3, 4),
    )
    table_two, accum_two = adagrad(table_one, accum_one, second)
    rel_part = dot(
        one_hot_t(rel_ids, relations.shape[0]), jnp.concatenate([first_rel, second_rel])
    ).astype(BF16)
    rel_total = sum_relations(rel_part, 5).astype(F32)
    new_rel, new_racc = adagrad(relations, rel_acc, rel_total)
    return (table_two, accum_two, new_rel, new_racc)


def solution(mesh):
    in_specs = (
        P(("grp", "shard"), None),
        P(("grp", "shard")),
        P(),
        P(),
        P(None, "grp", "shard", None),
        P(None, "grp", "shard", None),
        P(None, "grp", "shard", None, None),
        P(None, "grp", "shard", None),
        P(None, "grp", "shard"),
        P(None, "grp", "shard"),
    )
    out_specs = (P(("grp", "shard"), None), P(("grp", "shard")), P(), P())
    return jax.shard_map(
        per_device, mesh=mesh, in_specs=in_specs, out_specs=out_specs, check_vma=False
    )
```

```python
import functools
import jax
import jax.numpy as jnp
from jax import lax
from jax.experimental import pallas as pl
from jax.experimental.pallas import tpu as pltpu
from jax.sharding import PartitionSpec as P

LEARN_RATE = 0.3
MESH = pl.DeviceIdType.MESH
F32 = jnp.float32
BF16 = jnp.bfloat16
LANES = 256


def adagrad(table, accum, gradient):
    total = accum + jnp.mean(gradient * gradient, axis=-1)
    return (table - LEARN_RATE * gradient / jnp.sqrt(total)[..., None], total)


def dot(a, b):
    return jnp.dot(a, b, preferred_element_type=F32)


def hot(index, size):
    places = lax.broadcasted_iota(jnp.int32, (index.shape[0], size), 1)
    return jnp.where(places == index, 1.0, 0.0).astype(BF16)


def hot_t(index, size, first=0):
    places = lax.broadcasted_iota(jnp.int32, (size, index.shape[1]), 0) + first
    return jnp.where(places == index, 1.0, 0.0).astype(BF16)


def bucket_kernel(turn, groups, shards, edges, capacity, *refs):
    refs = list(refs)
    take = lambda n: [refs.pop(0) for _ in range(n)]
    table, relations, meta, requests = take(4)
    rel_prev = take(1)[0] if turn else None
    total_out, rel_out = take(2)
    asked_next = None if turn else take(1)[0]
    (asked, meta_t, own_negs, negs, sent, got, back, neg_send, neg_got, src_emb, rel_rows,
     query_bf, query_grad, src_grad, rel_grad, dst_grad, neg_acc, high, low) = take(19)
    if turn:
        half, rel_got_c, got_x, got_y, sum_x, sum_y, got_x2, got_y2, last, got_z = take(10)
    (req_send, req_recv, neg_send_sem, neg_recv_sem, row_send, row_recv, ngr_send, ngr_recv,
     grad_send, grad_recv, next_sem) = take(11)
    if turn:
        rel_send, rel_recv = take(2)

    rows, width = table.shape
    n_rel = relations.shape[0]
    n_own = own_negs.shape[0]
    n_neg = negs.shape[0]
    g, s = lax.axis_index("grp"), lax.axis_index("shard")
    next_g, prev_g = lax.rem(g + 1, groups), lax.rem(g + groups - 1, groups)
    to_g = prev_g if turn else g
    from_g = next_g if turn else g
    first = 0 if turn else 1
    tile = edges // 3
    chunk = lambda ref, i, size: ref.at[pl.ds(pl.multiple_of(i * size, 16), size)]

    x, y_hi, core = g // 4, lax.rem(g // 2, 2), lax.rem(g, 2)
    z, y_lo = s // 2, lax.rem(s, 2)
    y = y_hi * 2 + y_lo

    def device(x, y, z, core):
        return (x * 4 + (y // 2) * 2 + core, z * 2 + lax.rem(y, 2))

    x_at = lambda k: lax.rem(x + k, 4)
    y_at = lambda k: lax.rem(y + k, 4)
    z_at = lambda k: lax.rem(z + k, 8)
    x_dev = lambda k: device(x_at(k), y, z, core)
    y_dev = lambda k: device(x, y_at(k), z, core)
    z_dev = lambda k: device(x, y, z_at(k), core)
    core_dev = device(x, y, z, 1 - core)

    barrier = pltpu.get_barrier_semaphore()

    def greet(k, carry):
        source = lax.rem(s + shards - k, shards)
        pl.semaphore_signal(barrier, inc=1, device_id=(from_g, source), device_id_type=MESH)
        return carry

    lax.fori_loop(first, shards, greet, 0)
    greeted = shards - first
    if turn:
        others = [core_dev] + [x_dev(k) for k in (1, 2, 3)] + [y_dev(k) for k in (1, 2, 3)]
        others += [z_dev(k) for k in range(1, 8)]
    else:
        others = [(prev_g, s)]
    for other in others:
        pl.semaphore_signal(barrier, inc=1, device_id=other, device_id_type=MESH)
    greeted += len(others)

    meta_t[...] = jnp.transpose(meta[...])
    neg_col = jnp.transpose(requests[shards])[:n_own, turn : turn + 1]
    own_negs[...] = dot(hot(neg_col, rows), table[...]).astype(BF16)
    pl.semaphore_wait(barrier, greeted)

    def request_copy(k):
        target = lax.rem(s + k, shards)
        return pltpu.make_async_remote_copy(
            src_ref=requests.at[target], dst_ref=asked.at[s],
            send_sem=req_send.at[k], recv_sem=req_recv.at[k],
            device_id=(g, target), device_id_type=MESH,
        )

    def neg_copy(k):
        return pltpu.make_async_remote_copy(
            src_ref=own_negs, dst_ref=chunk(negs, s, n_own),
            send_sem=neg_send_sem.at[k], recv_sem=neg_recv_sem.at[k],
            device_id=(to_g, lax.rem(s + k, shards)), device_id_type=MESH,
        )

    def row_copy(k):
        target = lax.rem(s + k, shards)
        return pltpu.make_async_remote_copy(
            src_ref=chunk(sent, target, capacity), dst_ref=chunk(got, s, capacity),
            send_sem=row_send.at[k], recv_sem=row_recv.at[k],
            device_id=(to_g, target), device_id_type=MESH,
        )

    def neg_grad_copy(k):
        target = lax.rem(s + k, shards)
        return pltpu.make_async_remote_copy(
            src_ref=chunk(neg_send, target, n_own), dst_ref=chunk(neg_got, s, n_own),
            send_sem=ngr_send.at[k], recv_sem=ngr_recv.at[k],
            device_id=(from_g, target), device_id_type=MESH,
        )

    def grad_copy(k):
        target = lax.rem(s + k, shards)
        return pltpu.make_async_remote_copy(
            src_ref=chunk(sent, target, capacity), dst_ref=chunk(back, s, capacity),
            send_sem=grad_send.at[k], recv_sem=grad_recv.at[k],
            device_id=(from_g, target), device_id_type=MESH,
        )

    def each(begin, body):
        def step(k, carry):
            body(k)
            return carry

        lax.fori_loop(begin, shards, step, 0)

    if turn == 0:
        each(1, lambda k: request_copy(k).start())
        asked[s] = requests[s]
        asked[shards] = requests[shards]
        negs[pl.ds(pl.multiple_of(s * n_own, 16), n_own), :] = own_negs[...]
    else:
        asked[...] = requests[...]
    each(first, lambda k: neg_copy(k).start())

    if turn == 0:
        each(1, lambda k: request_copy(k).wait())
        forward = pltpu.make_async_remote_copy(
            src_ref=asked, dst_ref=asked_next, send_sem=next_sem.at[0], recv_sem=next_sem.at[1],
            device_id=(next_g, s), device_id_type=MESH,
        )
        forward.start()

    def answer(who):
        column = jnp.transpose(asked[who])[:capacity, turn : turn + 1]
        return dot(hot(column, rows), table[...]).astype(BF16)

    def send_rows(k):
        target = lax.rem(s + k, shards)
        sent[pl.ds(pl.multiple_of(target * capacity, 16), capacity), :] = answer(target)
        row_copy(k).start()

    each(first, send_rows)
    if turn == 0:
        got[pl.ds(pl.multiple_of(s * capacity, 16), capacity), :] = answer(s)

    def split(i, carry):
        at = pl.ds(i * 512, 512)
        value = relations[at, :]
        upper = value.astype(BF16)
        high[at, :] = upper
        low[at, :] = (value - upper.astype(F32)).astype(BF16)
        return carry

    lax.fori_loop(0, n_rel // 512, split, 0)

    def look(i, carry):
        at = pl.ds(pl.multiple_of(i * tile, 128), tile)
        columns = meta_t[at, :]
        emb = dot(hot(columns[:, 1:2], rows), table[...])
        picked = hot(columns[:, 3:4], n_rel)
        rel = dot(picked, high[...]) + dot(picked, low[...])
        src_emb[at, :] = emb.astype(BF16)
        rel_rows[at, :] = rel
        query_bf[at, :] = (emb * rel).astype(BF16)
        return carry

    lax.fori_loop(0, 3, look, 0)

    each(first, lambda k: neg_copy(k).wait())
    neg_acc[...] = jnp.zeros_like(neg_acc)

    def against_negatives(i, carry):
        at = pl.ds(pl.multiple_of(i * tile, 128), tile)
        query = query_bf[at, :]
        scores = lax.dot_general(
            query, negs[...], (((1,), (1,)), ((), ())), preferred_element_type=F32
        )
        live = meta_t[at, :][:, 2:3] > 0
        weight = jnp.where(live, (jnp.tanh(scores * 0.5) + 1.0) * (0.5 / n_neg), 0.0).astype(BF16)
        query_grad[at, :] = dot(weight, negs[...])
        neg_acc[...] += dot(jnp.transpose(query.astype(F32)).astype(BF16), weight)
        return carry

    lax.fori_loop(0, 3, against_negatives, 0)
    neg_send[...] = jnp.transpose(neg_acc[...]).astype(BF16)
    if turn == 0:
        own = pl.ds(pl.multiple_of(s * n_own, 16), n_own)
        neg_got[own, :] = neg_send[own, :]
    each(first, lambda k: neg_grad_copy(k).start())
    each(first, lambda k: row_copy(k).wait_recv())

    def positives(i, carry):
        at = pl.ds(pl.multiple_of(i * tile, 128), tile)
        columns = meta_t[at, :]
        emb = src_emb[at, :].astype(F32)
        rel = rel_rows[at, :]
        query = emb * rel
        dst = dot(hot(columns[:, 0:1], shards * capacity), got[...])
        positive = jnp.sum(query * dst, axis=1, keepdims=True)
        weight = jnp.where(columns[:, 2:3] > 0, (jnp.tanh(positive * -0.5) + 1.0) * -0.5, 0.0)
        grad = weight * dst + query_grad[at, :]
        src_grad[at, :] = (grad * rel).astype(BF16)
        rel_grad[at, :] = (grad * emb).astype(BF16)
        dst_grad[at, :] = (weight * query).astype(BF16)
        return carry

    lax.fori_loop(0, 3, positives, 0)

    def scatter_relations(begin, count):
        def step(i, carry):
            at = pl.multiple_of(begin + i * 512, 512)
            part = dot(hot_t(meta[3:4, :], 512, at), rel_grad[...])
            if turn:
                part = part + rel_prev[pl.ds(at, 512), :].astype(F32)
                half[pl.ds(at, 512), :] = part.astype(BF16)
            else:
                rel_out[pl.ds(at, 512), :] = part.astype(BF16)
            return carry

        lax.fori_loop(0, count // 512, step, 0)

    def send_grads():
        each(first, lambda k: row_copy(k).wait_send())

        def block(target):
            return dot(hot_t(meta[0:1, :], capacity, target * capacity), dst_grad[...]).astype(BF16)

        def send(k):
            target = lax.rem(s + k, shards)
            sent[pl.ds(pl.multiple_of(target * capacity, 16), capacity), :] = block(target)
            grad_copy(k).start()

        each(first, send)
        if turn == 0:
            back[pl.ds(pl.multiple_of(s * capacity, 16), capacity), :] = block(s)

    def scatter_sources():
        def step(i, carry):
            at = pl.multiple_of(i * 256, 256)
            total_out[pl.ds(at, 256), :] = dot(hot_t(meta[1:2, :], 256, at), src_grad[...])
            return carry

        lax.fori_loop(0, rows // 256, step, 0)

    def take_grads():
        each(first, lambda k: neg_grad_copy(k).wait())
        summed = neg_got[0:n_own, :].astype(F32)
        for k in range(1, shards):
            summed += neg_got[k * n_own : (k + 1) * n_own, :].astype(F32)
        upper = summed.astype(BF16)
        lower = (summed - upper.astype(F32)).astype(BF16)
        picked = hot_t(asked[shards][turn : turn + 1, :n_own], rows)
        total_out[...] += dot(picked, upper) + dot(picked, lower)

        def add(who):
            picked = hot_t(asked[who][turn : turn + 1, :capacity], rows)
            block = back[pl.ds(pl.multiple_of(who * capacity, 16), capacity), :]
            total_out[...] += dot(picked, block)

        if turn == 0:
            add(s)

        def take_one(k):
            grad_copy(k).wait()
            add(lax.rem(s + shards - k, shards))

        each(first, take_one)

    if turn == 0:
        send_grads()
        scatter_sources()
        scatter_relations(0, n_rel)
        take_grads()
        forward.wait()
        return

    n_half, n_quarter = n_rel // 2, n_rel // 4
    big, small, least = n_quarter // 4, n_quarter // 16, n_rel // 256
    mine, theirs = core * n_half, (1 - core) * n_half

    def rel_copy(src, dst, sem, where):
        return pltpu.make_async_remote_copy(
            src_ref=src, dst_ref=dst, send_sem=rel_send.at[sem], recv_sem=rel_recv.at[sem],
            device_id=where, device_id_type=MESH,
        )

    span = lambda ref, at, size: ref.at[pl.ds(pl.multiple_of(at, 16), size)]

    def run(copies):
        for copy in copies:
            copy.start()
        return copies

    def finish(copies):
        for copy in copies:
            copy.wait()

    scatter_relations(theirs, n_half)
    copies = run([rel_copy(span(half, theirs, n_half), rel_got_c, 0, core_dev)])
    send_grads()
    scatter_relations(mine, n_half)
    finish(copies)

    def add_core(i, carry):
        at = pl.multiple_of(i * 256, 256)
        value = half[pl.ds(mine + at, 256), :].astype(F32) + rel_got_c[pl.ds(at, 256), :].astype(F32)
        rel_got_c[pl.ds(at, 256), :] = value.astype(BF16)
        return carry

    lax.fori_loop(0, n_half // 256, add_core, 0)
    chip = rel_got_c
    copies = run(
        [rel_copy(span(chip, x_at(k) * big, big), got_x.at[k - 1], k, x_dev(k)) for k in (1, 2, 3)]
        + [
            rel_copy(span(chip, n_quarter + y_at(k) * big, big), got_y.at[k - 1], 3 + k, y_dev(k))
            for k in (1, 2, 3)
        ]
    )
    scatter_sources()
    finish(copies)

    def sum_of(ref, at, size, arrived):
        value = ref[pl.ds(pl.multiple_of(at, 16), size), :].astype(F32)
        for k in range(arrived.shape[0]):
            value += arrived[k].astype(F32)
        return value.astype(BF16)

    sum_x[...] = sum_of(chip, x * big, big, got_x)
    sum_y[...] = sum_of(chip, n_quarter + y * big, big, got_y)
    copies = run(
        [rel_copy(span(sum_x, y_at(k) * small, small), got_y2.at[k - 1], 6 + k, y_dev(k)) for k in (1, 2, 3)]
        + [rel_copy(span(sum_y, x_at(k) * small, small), got_x2.at[k - 1], 9 + k, x_dev(k)) for k in (1, 2, 3)]
    )
    finish(copies)
    last[0:small, :] = sum_of(sum_x, y * small, small, got_y2)
    last[small : 2 * small, :] = sum_of(sum_y, x * small, small, got_x2)
    copies = run(
        [rel_copy(span(last, z_at(k) * least, least), got_z.at[k - 1], 12 + k, z_dev(k)) for k in range(1, 8)]
    )
    finish(copies)
    side = z // 4
    at_x = mine + x * big + y * small
    at_y = mine + n_quarter + y * big + x * small
    at_z = at_x + side * (at_y - at_x) + lax.rem(z, 4) * least
    rel_out[pl.ds(pl.multiple_of(at_z, 16), least), :] = sum_of(last, z * least, least, got_z)
    same = lambda at, size: [span(rel_out, at, size)] * 2
    finish(run([rel_copy(*same(at_z, least), 19 + k, z_dev(k)) for k in range(1, 8)]))
    finish(
        run(
            [rel_copy(*same(at_x, small), 26 + k, y_dev(k)) for k in (1, 2, 3)]
            + [rel_copy(*same(at_y, small), 29 + k, x_dev(k)) for k in (1, 2, 3)]
        )
    )
    copies = run(
        [rel_copy(*same(mine + x * big, big), 32 + k, x_dev(k)) for k in (1, 2, 3)]
        + [rel_copy(*same(mine + n_quarter + y * big, big), 35 + k, y_dev(k)) for k in (1, 2, 3)]
    )
    take_grads()
    finish(copies)
    finish(run([rel_copy(*same(mine, n_half), 39, core_dev)]))


def bucket(turn, table, relations, meta, requests, rel_prev, groups, shards, capacity):
    rows, width = table.shape
    n_rel, edges = relations.shape[0], meta.shape[1]
    n_own = 64
    n_neg = shards * n_own
    bf = lambda *shape: pltpu.VMEM(shape + (width,), BF16)
    f32 = lambda *shape: pltpu.VMEM(shape + (width,), F32)
    scratch = [
        pltpu.VMEM(requests.shape, jnp.int32),
        pltpu.VMEM((edges, 8), jnp.int32),
        bf(n_own), bf(n_neg),
        bf(shards * capacity), bf(shards * capacity), bf(shards * capacity),
        bf(n_neg), bf(n_neg),
        bf(edges), f32(edges), bf(edges), f32(edges), bf(edges), bf(edges), bf(edges),
        pltpu.VMEM((width, n_neg), F32),
        bf(n_rel), bf(n_rel),
    ]
    if turn:
        scratch += [
            bf(n_rel), bf(n_rel // 2),
            bf(3, n_rel // 16), bf(3, n_rel // 16), bf(n_rel // 16), bf(n_rel // 16),
            bf(3, n_rel // 64), bf(3, n_rel // 64), bf(n_rel // 32), bf(7, n_rel // 256),
        ]
    scratch += [pltpu.SemaphoreType.DMA((shards,))] * 10 + [pltpu.SemaphoreType.DMA((2,))]
    if turn:
        scratch += [pltpu.SemaphoreType.DMA((40,))] * 2
    out = [
        jax.ShapeDtypeStruct((rows, width), F32),
        jax.ShapeDtypeStruct((n_rel, width), BF16),
    ]
    if turn == 0:
        out.append(jax.ShapeDtypeStruct(requests.shape, jnp.int32))
    args = [table, relations, meta, requests] + ([rel_prev] if turn else [])
    return pl.pallas_call(
        functools.partial(bucket_kernel, turn, groups, shards, edges, capacity),
        out_shape=out,
        in_specs=[pl.BlockSpec(memory_space=pltpu.VMEM)] * len(args),
        out_specs=[pl.BlockSpec(memory_space=pltpu.VMEM)] * len(out),
        scratch_shapes=scratch,
        compiler_params=pltpu.CompilerParams(
            collective_id=turn, has_side_effects=True, vmem_limit_bytes=56 << 20
        ),
        name="bucket_one" if turn else "bucket_zero",
    )(*args)


def one_hot(index, size):
    return (index[:, None] == jnp.arange(size, dtype=jnp.int32)[None, :]).astype(BF16)


def one_hot_t(index, size):
    return (jnp.arange(size, dtype=jnp.int32)[:, None] == index[None, :]).astype(BF16)


def plan(owners, dst_rows, shards, capacity):
    edges = owners.shape[0]
    position = jnp.arange(edges, dtype=jnp.int32)
    chosen = one_hot(owners, shards)
    before = (position[None, :] < position[:, None]).astype(BF16)
    ranks = jnp.sum(dot(before, chosen) * chosen.astype(F32), axis=1).astype(jnp.int32)
    chosen_t = one_hot_t(owners, shards)
    by_rank = one_hot(ranks, LANES)
    upper = dot(chosen_t * (dst_rows // 32).astype(BF16)[None, :], by_rank)
    lower = dot(chosen_t * (dst_rows % 32).astype(BF16)[None, :], by_rank)
    return owners * capacity + ranks, (upper * 32 + lower).astype(jnp.int32)


def per_device(
    entities, row_acc, relations, rel_acc, src_row, rel_id, dst_owner, dst_row, neg_rows, lengths
):
    groups, shards = lax.axis_size("grp"), lax.axis_size("shard")
    edges = src_row.shape[-1]
    capacity = 2 * edges // shards
    metas, requests = [], []
    for turn in range(2):
        slot, request = plan(dst_owner[turn, 0, 0, :, 0], dst_row[turn, 0, 0], shards, capacity)
        live = (jnp.arange(edges, dtype=jnp.int32) < lengths[turn, 0, 0]).astype(jnp.int32)
        metas.append(
            jnp.pad(
                jnp.stack([slot, src_row[turn, 0, 0], live, rel_id[turn, 0, 0]]), ((0, 4), (0, 0))
            )
        )
        named = jnp.pad(neg_rows[turn], ((0, 0), (0, LANES - neg_rows.shape[-1])))
        requests.append(jnp.concatenate([request, named]))
    requests = jnp.pad(jnp.stack(requests, axis=1), ((0, 0), (0, 6), (0, 0)))
    first, rel_part, asked = bucket(
        0, entities.astype(BF16), relations, metas[0], requests, None, groups, shards, capacity
    )
    table_one, accum_one = adagrad(entities, row_acc, first)
    second, rel_total = bucket(
        1, table_one.astype(BF16), relations, metas[1], asked, rel_part, groups, shards, capacity
    )
    table_two, accum_two = adagrad(table_one, accum_one, second)
    new_rel, new_racc = adagrad(relations, rel_acc, rel_total.astype(F32))
    return (table_two, accum_two, new_rel, new_racc)


def solution(mesh):
    in_specs = (
        P(("grp", "shard"), None),
        P(("grp", "shard")),
        P(),
        P(),
        P(None, "grp", "shard", None),
        P(None, "grp", "shard", None),
        P(None, "grp", "shard", None, None),
        P(None, "grp", "shard", None),
        P(None, "grp", "shard"),
        P(None, "grp", "shard"),
    )
    out_specs = (P(("grp", "shard"), None), P(("grp", "shard")), P(), P())
    return jax.shard_map(
        per_device, mesh=mesh, in_specs=in_specs, out_specs=out_specs, check_vma=False
    )
```

```python
import functools
import jax
import jax.numpy as jnp
from jax import lax
from jax.experimental import pallas as pl
from jax.experimental.pallas import tpu as pltpu
from jax.sharding import PartitionSpec as P

LEARN_RATE = 0.3
MESH = pl.DeviceIdType.MESH
F32 = jnp.float32
BF16 = jnp.bfloat16
LANES = 256


def adagrad(table, accum, gradient):
    total = accum + jnp.mean(gradient * gradient, axis=-1)
    return (table - LEARN_RATE * gradient / jnp.sqrt(total)[..., None], total)


def dot(a, b):
    return jnp.dot(a, b, preferred_element_type=F32)


def hot(index, size):
    places = lax.broadcasted_iota(jnp.int32, (index.shape[0], size), 1)
    return jnp.where(places == index, 1.0, 0.0).astype(BF16)


def hot_t(index, size, first=0):
    places = lax.broadcasted_iota(jnp.int32, (size, index.shape[1]), 0) + first
    return jnp.where(places == index, 1.0, 0.0).astype(BF16)


def train_kernel(groups, shards, edges, capacity, n_own, *refs):
    (entities, row_acc, relations, src_row, rel_id, dst_owner, dst_row, neg_rows, lengths,
     table, acc_out, rel_out,
     meta, meta_t, requests, asked, asked_next, asked_t, chunks, high, low, table_bf, acc_t,
     own_negs, negs_2, sent, got_2, back_2, neg_send, pair_got_2, pair_sum, neg_got_2,
     src_emb, rel_rows_2, query_bf, query_grad, src_grad, rel_grad, dst_grad, neg_acc, total,
     by_slot, by_slot_t, by_asked_t, by_rel_t,
     half, rel_got_c, got_x, got_y, sum_x, sum_y, got_x2, got_y2, last, got_z,
     chunk_sem, req_send, req_recv, neg_sems, row_send, row_recv, pair_sems,
     ngr_send, ngr_recv, grad_send, grad_recv, next_sem, rel_send, rel_recv) = refs

    rows, width = table.shape
    n_rel = relations.shape[0]
    n_neg = shards * n_own
    n_side = n_neg // 2
    depth = shards // 2
    slots = shards * capacity
    g, s = lax.axis_index("grp"), lax.axis_index("shard")
    next_g, prev_g = lax.rem(g + 1, groups), lax.rem(g + groups - 1, groups)
    tile = edges // 3
    chunk = lambda ref, i, size: ref.at[pl.ds(pl.multiple_of(i * size, 16), size)]
    span = lambda ref, at, size: ref.at[pl.ds(pl.multiple_of(at, 16), size)]

    x, y_hi, core = g // 4, lax.rem(g // 2, 2), lax.rem(g, 2)
    z, y_lo = s // 2, lax.rem(s, 2)
    y = y_hi * 2 + y_lo
    pair_s = z * 2 + 1 - y_lo
    along = lambda k: lax.rem(z + k, depth) * 2 + y_lo

    def device(x, y, z, core):
        return (x * 4 + (y // 2) * 2 + core, z * 2 + lax.rem(y, 2))

    x_at = lambda k: lax.rem(x + k, 4)
    y_at = lambda k: lax.rem(y + k, 4)
    z_at = lambda k: lax.rem(z + k, 8)
    x_dev = lambda k: device(x_at(k), y, z, core)
    y_dev = lambda k: device(x, y_at(k), z, core)
    z_dev = lambda k: device(x, y, z_at(k), core)
    core_dev = device(x, y, z, 1 - core)

    def each(begin, end, body):
        def step(k, carry):
            body(k)
            return carry

        lax.fori_loop(begin, end, step, 0)

    barrier = pltpu.get_barrier_semaphore()

    def greet(where):
        pl.semaphore_signal(barrier, inc=1, device_id=where, device_id_type=MESH)

    each(1, shards, lambda k: greet((g, lax.rem(s + shards - k, shards))))
    others = [(prev_g, s), core_dev] + [x_dev(k) for k in (1, 2, 3)] + [y_dev(k) for k in (1, 2, 3)]
    for other in others:
        greet(other)

    rel_steps = n_rel // chunks.shape[1]

    def load(i):
        return pltpu.make_async_copy(
            chunk(relations, i, chunks.shape[1]), chunks.at[i % 2], chunk_sem.at[i % 2]
        )

    load(0).start()
    load(1).start()

    for t in range(2):
        meta[t : t + 1, :] = dst_owner[t, 0]
        meta[2 + t : 3 + t, :] = src_row[t, 0]
        meta[4 + t : 5 + t, :] = rel_id[t, 0]
    meta[6:8, :] = jnp.zeros((2, edges), jnp.int32)
    meta_t[...] = jnp.transpose(meta[...])
    requests[...] = jnp.zeros_like(requests)
    lower_tri = jnp.where(
        lax.broadcasted_iota(jnp.int32, (128, 128), 1)
        < lax.broadcasted_iota(jnp.int32, (128, 128), 0),
        1.0,
        0.0,
    ).astype(BF16)
    shard_rows = lax.broadcasted_iota(jnp.int32, (shards, 128), 0)
    for t in range(2):
        base = jnp.zeros((1, 128), F32)
        upper = jnp.zeros((shards, LANES), F32)
        lower = jnp.zeros((shards, LANES), F32)
        for b in range(edges // 128):
            at = slice(b * 128, b * 128 + 128)
            owner = meta_t[at, t : t + 1]
            chosen = hot(owner, 128)
            chosen_f = chosen.astype(F32)
            count = dot(lower_tri, chosen) + base
            rank = jnp.sum(count * chosen_f, axis=1, keepdims=True).astype(jnp.int32)
            base = base + jnp.sum(chosen_f, axis=0, keepdims=True)
            meta_t[at, 6 + t : 7 + t] = owner * capacity + rank
            by_rank = hot(rank, LANES)
            row = dst_row[t, 0, :, at]
            named = meta[t : t + 1, at] == shard_rows
            part = lambda value: dot(jnp.where(named, value.astype(F32), 0.0).astype(BF16), by_rank)
            upper = upper + part(lax.shift_right_logical(row, 5))
            lower = lower + part(row & 31)
        asking = (upper * 32.0 + lower).astype(jnp.int32)
        for o in range(shards):
            requests[o, t : t + 1, :] = asking[o : o + 1, :]
        requests[shards, t : t + 1, :n_own] = neg_rows[t]
    meta[...] = jnp.transpose(meta_t[...])
    table[...] = entities[...]
    table_bf[...] = entities[...].astype(BF16)
    acc_t[...] = jnp.transpose(row_acc[...])

    def name_negatives(t):
        column = jnp.transpose((asked_next if t else requests)[shards])[:n_own, t : t + 1]
        own_negs[...] = dot(hot(column, rows), table_bf[...]).astype(BF16)

    name_negatives(0)
    pl.semaphore_wait(barrier, shards - 1 + len(others))

    def request_copy(k):
        target = lax.rem(s + k, shards)
        return pltpu.make_async_remote_copy(
            src_ref=requests.at[target], dst_ref=asked.at[s],
            send_sem=req_send.at[k], recv_sem=req_recv.at[k],
            device_id=(g, target), device_id_type=MESH,
        )

    forward = pltpu.make_async_remote_copy(
        src_ref=asked, dst_ref=asked_next, send_sem=next_sem.at[0], recv_sem=next_sem.at[1],
        device_id=(next_g, s), device_id_type=MESH,
    )

    def look_relations(t):
        def step(i, carry):
            at = pl.ds(pl.multiple_of(i * tile, 128), tile)
            picked = hot(meta_t[at, :][:, 4 + t : 5 + t], n_rel)
            rel_rows_2[t, at, :] = dot(picked, high[...]) + dot(picked, low[...])
            return carry

        lax.fori_loop(0, 3, step, 0)

    def round_of(t):
        to_g = prev_g if t else g
        from_g = next_g if t else g
        first = 0 if t else 1
        negs, got, back = negs_2.at[t], got_2.at[t], back_2.at[t]
        pair_got, neg_got, rel_rows = pair_got_2.at[t], neg_got_2.at[t], rel_rows_2.at[t]
        wanted = asked_next if t else asked
        limit = lengths[t, 0, 0]

        def live(i):
            place = lax.broadcasted_iota(jnp.int32, (tile, 1), 0) + i * tile
            return place < limit

        my_block = y_lo * depth + z

        def neg_copy(k):
            return pltpu.make_async_remote_copy(
                src_ref=own_negs, dst_ref=chunk(negs, my_block, n_own),
                send_sem=neg_sems.at[t, 0, k], recv_sem=neg_sems.at[t, 1, k],
                device_id=(to_g, along(k)), device_id_type=MESH,
            )

        neg_pair = pltpu.make_async_remote_copy(
            src_ref=chunk(negs, y_lo, n_side), dst_ref=chunk(negs, y_lo, n_side),
            send_sem=neg_sems.at[t, 0, depth], recv_sem=neg_sems.at[t, 1, depth],
            device_id=(g, pair_s), device_id_type=MESH,
        )

        def row_copy(k):
            target = lax.rem(s + k, shards)
            return pltpu.make_async_remote_copy(
                src_ref=chunk(sent, target, capacity), dst_ref=chunk(got, s, capacity),
                send_sem=row_send.at[t, k], recv_sem=row_recv.at[t, k],
                device_id=(to_g, target), device_id_type=MESH,
            )

        pair_copy = pltpu.make_async_remote_copy(
            src_ref=chunk(neg_send, 1 - y_lo, n_side), dst_ref=pair_got,
            send_sem=pair_sems.at[t, 0], recv_sem=pair_sems.at[t, 1],
            device_id=(g, pair_s), device_id_type=MESH,
        )

        def neg_grad_copy(k):
            return pltpu.make_async_remote_copy(
                src_ref=chunk(pair_sum, z_at(k), n_own), dst_ref=chunk(neg_got, z, n_own),
                send_sem=ngr_send.at[t, k], recv_sem=ngr_recv.at[t, k],
                device_id=(from_g, along(k)), device_id_type=MESH,
            )

        def grad_copy(k):
            target = lax.rem(s + k, shards)
            return pltpu.make_async_remote_copy(
                src_ref=chunk(sent, target, capacity), dst_ref=chunk(back, s, capacity),
                send_sem=grad_send.at[t, k], recv_sem=grad_recv.at[t, k],
                device_id=(from_g, target), device_id_type=MESH,
            )

        if t == 0:
            each(1, shards, lambda k: request_copy(k).start())
            asked[s] = requests[s]
            asked[shards] = requests[shards]
            negs[pl.ds(pl.multiple_of(my_block * n_own, 16), n_own), :] = own_negs[...]
        else:
            forward.wait()
            name_negatives(1)
        each(first, depth, lambda k: neg_copy(k).start())

        if t == 0:
            for i in range(rel_steps):
                load(i).wait()
                value = chunks[i % 2]
                top = value.astype(BF16)
                at = slice(i * chunks.shape[1], (i + 1) * chunks.shape[1])
                high[at, :] = top
                low[at, :] = (value - top.astype(F32)).astype(BF16)
                if i + 2 < rel_steps:
                    load(i + 2).start()
            each(1, shards, lambda k: request_copy(k).wait())
            forward.start()

        def answer(who):
            columns = jnp.transpose(wanted[who])[:capacity, :]
            asked_t[pl.ds(pl.multiple_of(who * capacity, 16), capacity), :] = columns
            return dot(hot(columns[:, t : t + 1], rows), table_bf[...]).astype(BF16)

        def send_rows(k):
            target = lax.rem(s + k, shards)
            sent[pl.ds(pl.multiple_of(target * capacity, 16), capacity), :] = answer(target)
            row_copy(k).start()

        each(first, shards, send_rows)
        if t == 0:
            got[pl.ds(pl.multiple_of(s * capacity, 16), capacity), :] = answer(s)
        each(first, depth, lambda k: neg_copy(k).wait())
        neg_pair.start()

        if t == 0:
            look_relations(0)

        def look_sources(i, carry):
            at = pl.ds(pl.multiple_of(i * tile, 128), tile)
            emb = dot(hot(meta_t[at, :][:, 2 + t : 3 + t], rows), table_bf[...])
            src_emb[at, :] = emb.astype(BF16)
            query_bf[at, :] = (emb * rel_rows[at, :]).astype(BF16)
            return carry

        lax.fori_loop(0, 3, look_sources, 0)

        neg_pair.wait()
        neg_acc[...] = jnp.zeros_like(neg_acc)

        def against_negatives(i, carry):
            at = pl.ds(pl.multiple_of(i * tile, 128), tile)
            query = query_bf[at, :]
            scores = lax.dot_general(
                query, negs[...], (((1,), (1,)), ((), ())), preferred_element_type=F32
            )
            weight = jnp.where(
                live(i), (jnp.tanh(scores * 0.5) + 1.0) * (0.5 / n_neg), 0.0
            ).astype(BF16)
            query_grad[at, :] = dot(weight, negs[...])
            neg_acc[...] += dot(jnp.transpose(query.astype(F32)).astype(BF16), weight)
            return carry

        lax.fori_loop(0, 3, against_negatives, 0)
        neg_send[...] = jnp.transpose(neg_acc[...]).astype(BF16)
        pair_copy.start()

        def mark_slots(i):
            at = pl.ds(pl.multiple_of(i * 128, 128), 128)
            by_slot[at, :] = hot(meta_t[at, :][:, 6 + t : 7 + t], slots)

        each(0, edges // 128, mark_slots)

        pair_copy.wait()
        mine_side = pl.ds(pl.multiple_of(y_lo * n_side, 16), n_side)
        pair_sum[...] = (neg_send[mine_side, :].astype(F32) + pair_got[...].astype(F32)).astype(BF16)
        if t == 0:
            own = pl.ds(pl.multiple_of(z * n_own, 16), n_own)
            neg_got[own, :] = pair_sum[own, :]
        each(first, depth, lambda k: neg_grad_copy(k).start())

        def mark_slots_t(i):
            at = pl.multiple_of(i * 128, 128)
            by_slot_t[pl.ds(at, 128), :] = hot_t(meta[6 + t : 7 + t, :], 128, at)

        each(0, slots // 128, mark_slots_t)
        asked_rows = jnp.transpose(asked_t[...])[t : t + 1, :]

        def mark_asked(i):
            at = pl.multiple_of(i * 128, 128)
            by_asked_t[pl.ds(at, 128), :] = hot_t(asked_rows, 128, at)

        each(0, rows // 128, mark_asked)

        n_half, n_quarter = n_rel // 2, n_rel // 4
        mine, theirs = core * n_half, (1 - core) * n_half
        if t:

            def mark_relations(i):
                at = pl.multiple_of(i * 128, 128)
                by_rel_t[pl.ds(at, 128), :] = hot_t(meta[4 + t : 5 + t, :], 128, theirs + at)

            each(0, n_half // 128, mark_relations)

        each(first, shards, lambda k: row_copy(k).wait_recv())

        def positives(i, carry):
            at = pl.ds(pl.multiple_of(i * tile, 128), tile)
            emb = src_emb[at, :].astype(F32)
            rel = rel_rows[at, :]
            query = emb * rel
            dst = dot(by_slot[at, :], got[...])
            positive = jnp.sum(query * dst, axis=1, keepdims=True)
            weight = jnp.where(live(i), (jnp.tanh(positive * -0.5) + 1.0) * -0.5, 0.0)
            grad = weight * dst + query_grad[at, :]
            src_grad[at, :] = (grad * rel).astype(BF16)
            rel_grad[at, :] = (grad * emb).astype(BF16)
            dst_grad[at, :] = (weight * query).astype(BF16)
            return carry

        lax.fori_loop(0, 3, positives, 0)

        def send_grads():
            each(first, shards, lambda k: row_copy(k).wait_send())

            def block(target):
                at = pl.ds(pl.multiple_of(target * capacity, 16), capacity)
                return dot(by_slot_t[at, :], dst_grad[...]).astype(BF16)

            def send(k):
                target = lax.rem(s + k, shards)
                sent[pl.ds(pl.multiple_of(target * capacity, 16), capacity), :] = block(target)
                grad_copy(k).start()

            each(first, shards, send)
            if t == 0:
                back[pl.ds(pl.multiple_of(s * capacity, 16), capacity), :] = block(s)

        def scatter_sources():
            def step(i):
                at = pl.multiple_of(i * 256, 256)
                total[pl.ds(at, 256), :] = dot(hot_t(meta[2 + t : 3 + t, :], 256, at), src_grad[...])

            each(0, rows // 256, step)

        def take_grads():
            each(first, depth, lambda k: neg_grad_copy(k).wait())
            summed = neg_got[0:n_own, :].astype(F32)
            for k in range(1, depth):
                summed += neg_got[k * n_own : (k + 1) * n_own, :].astype(F32)
            upper = summed.astype(BF16)
            lower = (summed - upper.astype(F32)).astype(BF16)
            picked = hot_t(wanted[shards][t : t + 1, :n_own], rows)
            total[...] += dot(picked, upper) + dot(picked, lower)
            each(first, shards, lambda k: grad_copy(k).wait())
            for i in range(rows // 128):
                at = slice(i * 128, i * 128 + 128)
                grad = total[at, :] + dot(by_asked_t[at, :], back[...])
                acc = acc_t[:, i : i + 1] + jnp.sum(grad * grad, axis=1, keepdims=True) * (1.0 / width)
                fresh = table[at, :] - LEARN_RATE * grad / jnp.sqrt(acc)
                acc_t[:, i : i + 1] = acc
                table[at, :] = fresh
                if t == 0:
                    table_bf[at, :] = fresh.astype(BF16)

        if t == 0:
            send_grads()
            scatter_sources()

            def scatter(i):
                at = pl.multiple_of(i * 512, 512)
                part = dot(hot_t(meta[4:5, :], 512, at), rel_grad[...])
                half[pl.ds(at, 512), :] = part.astype(BF16)

            each(0, n_rel // 512, scatter)
            look_relations(1)
            take_grads()
            return

        big, small, least = n_quarter // 4, n_quarter // 16, n_rel // 256

        def rel_copy(src, dst, sem, where):
            return pltpu.make_async_remote_copy(
                src_ref=src, dst_ref=dst, send_sem=rel_send.at[sem], recv_sem=rel_recv.at[sem],
                device_id=where, device_id_type=MESH,
            )

        def run(copies):
            for copy in copies:
                copy.start()
            return copies

        def finish(copies):
            for copy in copies:
                copy.wait()

        def scatter_theirs(i):
            at = pl.multiple_of(i * 512, 512)
            where = pl.ds(pl.multiple_of(theirs + at, 512), 512)
            part = dot(by_rel_t[pl.ds(at, 512), :], rel_grad[...])
            half[where, :] = (half[where, :].astype(F32) + part).astype(BF16)

        def scatter_mine(i):
            at = pl.multiple_of(mine + i * 512, 512)
            part = dot(hot_t(meta[5:6, :], 512, at), rel_grad[...])
            half[pl.ds(at, 512), :] = (half[pl.ds(at, 512), :].astype(F32) + part).astype(BF16)

        each(0, n_half // 512, scatter_theirs)
        copies = run([rel_copy(span(half, theirs, n_half), rel_got_c, 0, core_dev)])
        send_grads()
        each(0, n_half // 512, scatter_mine)
        finish(copies)

        def add_core(i):
            at = pl.multiple_of(i * 256, 256)
            mine_at = pl.ds(pl.multiple_of(mine + at, 256), 256)
            value = half[mine_at, :].astype(F32) + rel_got_c[pl.ds(at, 256), :].astype(F32)
            rel_got_c[pl.ds(at, 256), :] = value.astype(BF16)

        each(0, n_half // 256, add_core)
        chip = rel_got_c
        copies = run(
            [rel_copy(span(chip, x_at(k) * big, big), got_x.at[k - 1], k, x_dev(k)) for k in (1, 2, 3)]
            + [
                rel_copy(span(chip, n_quarter + y_at(k) * big, big), got_y.at[k - 1], 3 + k, y_dev(k))
                for k in (1, 2, 3)
            ]
        )
        scatter_sources()
        finish(copies)

        def sum_of(ref, at, size, arrived):
            value = ref[pl.ds(pl.multiple_of(at, 16), size), :].astype(F32)
            for k in range(arrived.shape[0]):
                value += arrived[k].astype(F32)
            return value.astype(BF16)

        sum_x[...] = sum_of(chip, x * big, big, got_x)
        sum_y[...] = sum_of(chip, n_quarter + y * big, big, got_y)
        copies = run(
            [rel_copy(span(sum_x, y_at(k) * small, small), got_y2.at[k - 1], 6 + k, y_dev(k)) for k in (1, 2, 3)]
            + [rel_copy(span(sum_y, x_at(k) * small, small), got_x2.at[k - 1], 9 + k, x_dev(k)) for k in (1, 2, 3)]
        )
        finish(copies)
        last[0:small, :] = sum_of(sum_x, y * small, small, got_y2)
        last[small : 2 * small, :] = sum_of(sum_y, x * small, small, got_x2)
        copies = run(
            [rel_copy(span(last, z_at(k) * least, least), got_z.at[k - 1], 12 + k, z_dev(k)) for k in range(1, 8)]
        )
        finish(copies)
        side = z // 4
        at_x = mine + x * big + y * small
        at_y = mine + n_quarter + y * big + x * small
        at_z = at_x + side * (at_y - at_x) + lax.rem(z, 4) * least
        rel_out[pl.ds(pl.multiple_of(at_z, 16), least), :] = sum_of(last, z * least, least, got_z)
        same = lambda at, size: [span(rel_out, at, size)] * 2
        finish(run([rel_copy(*same(at_z, least), 19 + k, z_dev(k)) for k in range(1, 8)]))
        finish(
            run(
                [rel_copy(*same(at_x, small), 26 + k, y_dev(k)) for k in (1, 2, 3)]
                + [rel_copy(*same(at_y, small), 29 + k, x_dev(k)) for k in (1, 2, 3)]
            )
        )
        copies = run(
            [rel_copy(*same(mine + x * big, big), 32 + k, x_dev(k)) for k in (1, 2, 3)]
            + [rel_copy(*same(mine + n_quarter + y * big, big), 35 + k, y_dev(k)) for k in (1, 2, 3)]
        )
        finish(copies)
        copies = run([rel_copy(*same(mine, n_half), 39, core_dev)])
        take_grads()
        finish(copies)

    round_of(0)
    round_of(1)
    acc_out[...] = jnp.transpose(acc_t[...])


def train(entities, row_acc, relations, src_row, rel_id, dst_owner, dst_row, neg_rows, lengths):
    groups, shards = lax.axis_size("grp"), lax.axis_size("shard")
    rows, width = entities.shape
    n_rel, edges, n_own = relations.shape[0], src_row.shape[-1], neg_rows.shape[-1]
    capacity = 2 * edges // shards
    n_neg, slots, depth = shards * n_own, shards * capacity, shards // 2
    bf = lambda *shape: pltpu.VMEM(shape + (width,), BF16)
    f32 = lambda *shape: pltpu.VMEM(shape + (width,), F32)
    i32 = lambda *shape: pltpu.VMEM(shape, jnp.int32)
    sems = lambda *shape: pltpu.SemaphoreType.DMA(shape)
    scratch = [
        i32(8, edges), i32(edges, 8),
        i32(shards + 1, 8, LANES), i32(shards + 1, 8, LANES), i32(shards + 1, 8, LANES), i32(slots, 8),
        f32(2, 512), bf(n_rel), bf(n_rel), bf(rows), pltpu.VMEM((rows // 8, 8), F32),
        bf(n_own), bf(2, n_neg), bf(slots), bf(2, slots), bf(2, slots),
        bf(n_neg), bf(2, n_neg // 2), bf(n_neg // 2), bf(2, n_neg // 2),
        bf(edges), f32(2, edges), bf(edges), f32(edges), bf(edges), bf(edges), bf(edges),
        pltpu.VMEM((width, n_neg), F32), f32(rows),
        pltpu.VMEM((edges, slots), BF16), pltpu.VMEM((slots, edges), BF16),
        pltpu.VMEM((rows, slots), BF16), pltpu.VMEM((n_rel // 2, edges), BF16),
        bf(n_rel), bf(n_rel // 2),
        bf(3, n_rel // 16), bf(3, n_rel // 16), bf(n_rel // 16), bf(n_rel // 16),
        bf(3, n_rel // 64), bf(3, n_rel // 64), bf(n_rel // 32), bf(7, n_rel // 256),
        sems(2), sems(shards), sems(shards), sems(2, 2, depth + 1),
        sems(2, shards), sems(2, shards), sems(2, 2),
        sems(2, depth), sems(2, depth), sems(2, shards), sems(2, shards),
        sems(2), sems(40), sems(40),
    ]
    vmem = pl.BlockSpec(memory_space=pltpu.VMEM)
    return pl.pallas_call(
        functools.partial(train_kernel, groups, shards, edges, capacity, n_own),
        out_shape=[
            jax.ShapeDtypeStruct((rows, width), F32),
            jax.ShapeDtypeStruct((8, rows // 8), F32),
            jax.ShapeDtypeStruct((n_rel, width), BF16),
        ],
        in_specs=[vmem, vmem, pl.BlockSpec(memory_space=pl.ANY)] + [vmem] * 5
        + [pl.BlockSpec(memory_space=pltpu.SMEM)],
        out_specs=[vmem] * 3,
        scratch_shapes=scratch,
        compiler_params=pltpu.CompilerParams(
            collective_id=0, has_side_effects=True, vmem_limit_bytes=60 << 20
        ),
        name="train",
    )(
        entities, row_acc.reshape(8, rows // 8), relations, src_row, rel_id,
        dst_owner[..., 0], dst_row, neg_rows, lengths,
    )


def per_device(
    entities, row_acc, relations, rel_acc, src_row, rel_id, dst_owner, dst_row, neg_rows, lengths
):
    table, accum, rel_total = train(
        entities, row_acc, relations, src_row, rel_id, dst_owner, dst_row, neg_rows, lengths
    )
    new_rel, new_racc = adagrad(relations, rel_acc, rel_total.astype(F32))
    return (table, accum.reshape(-1), new_rel, new_racc)


def solution(mesh):
    in_specs = (
        P(("grp", "shard"), None),
        P(("grp", "shard")),
        P(),
        P(),
        P(None, "grp", "shard", None),
        P(None, "grp", "shard", None),
        P(None, "grp", "shard", None, None),
        P(None, "grp", "shard", None),
        P(None, "grp", "shard"),
        P(None, "grp", "shard"),
    )
    out_specs = (P(("grp", "shard"), None), P(("grp", "shard")), P(), P())
    return jax.shard_map(
        per_device, mesh=mesh, in_specs=in_specs, out_specs=out_specs, check_vma=False
    )
```

```python
import functools
import jax
import jax.numpy as jnp
from jax import lax
from jax.experimental import pallas as pl
from jax.experimental.pallas import tpu as pltpu
from jax.sharding import PartitionSpec as P

LEARN_RATE = 0.3
MESH = pl.DeviceIdType.MESH
F32 = jnp.float32
BF16 = jnp.bfloat16
LANES = 256


def adagrad(table, accum, gradient):
    total = accum + jnp.mean(gradient * gradient, axis=-1)
    return (table - LEARN_RATE * gradient / jnp.sqrt(total)[..., None], total)


def dot(a, b):
    return jnp.dot(a, b, preferred_element_type=F32)


def hot(index, size):
    places = lax.broadcasted_iota(jnp.int32, (index.shape[0], size), 1)
    return jnp.where(places == index, 1.0, 0.0).astype(BF16)


def hot_t(index, size, first=0):
    places = lax.broadcasted_iota(jnp.int32, (size, index.shape[1]), 0) + first
    return jnp.where(places == index, 1.0, 0.0).astype(BF16)


def train_kernel(groups, shards, edges, capacity, n_own, *refs):
    (entities, row_acc, relations, src_row, rel_id, dst_owner, dst_row, neg_rows, lengths,
     table, acc_out, rel_out,
     meta, meta_t, requests_2, asked_2, asked_next, asked_t, chunks, high, low, table_bf, acc_t,
     own_negs, negs_2, sent, queries, got_2, back_2, neg_send, pair_got_2, pair_sum, neg_got_2,
     src_emb, rel_rows_2, query_bf, query_grad, src_grad, rel_grad, neg_acc, total,
     by_slot, by_slot_t, by_asked_t, by_rel_t,
     half, rel_got_c, got_x, got_y, sum_x, sum_y, got_x2, got_y2, last, got_z,
     chunk_sem, req_send, req_recv, neg_sems, row_send, row_recv, pair_sems,
     ngr_send, ngr_recv, grad_send, grad_recv, next_sem, rel_send, rel_recv) = refs

    rows, width = table.shape
    n_rel = relations.shape[0]
    n_neg = shards * n_own
    n_side = n_neg // 2
    depth = shards // 2
    slots = shards * capacity
    g, s = lax.axis_index("grp"), lax.axis_index("shard")
    next_g, prev_g = lax.rem(g + 1, groups), lax.rem(g + groups - 1, groups)
    tile = edges // 3
    chunk = lambda ref, i, size: ref.at[pl.ds(pl.multiple_of(i * size, 16), size)]
    span = lambda ref, at, size: ref.at[pl.ds(pl.multiple_of(at, 16), size)]

    x, y_hi, core = g // 4, lax.rem(g // 2, 2), lax.rem(g, 2)
    z, y_lo = s // 2, lax.rem(s, 2)
    y = y_hi * 2 + y_lo
    pair_s = z * 2 + 1 - y_lo
    along = lambda k: lax.rem(z + k, depth) * 2 + y_lo

    def device(x, y, z, core):
        return (x * 4 + (y // 2) * 2 + core, z * 2 + lax.rem(y, 2))

    x_at = lambda k: lax.rem(x + k, 4)
    y_at = lambda k: lax.rem(y + k, 4)
    z_at = lambda k: lax.rem(z + k, 8)
    x_dev = lambda k: device(x_at(k), y, z, core)
    y_dev = lambda k: device(x, y_at(k), z, core)
    z_dev = lambda k: device(x, y, z_at(k), core)
    core_dev = device(x, y, z, 1 - core)

    def each(begin, end, body):
        def step(k, carry):
            body(k)
            return carry

        lax.fori_loop(begin, end, step, 0)

    barrier = pltpu.get_barrier_semaphore()

    def greet(where):
        pl.semaphore_signal(barrier, inc=1, device_id=where, device_id_type=MESH)

    each(1, shards, lambda k: greet((g, lax.rem(s + shards - k, shards))))
    others = [(prev_g, s), core_dev] + [x_dev(k) for k in (1, 2, 3)] + [y_dev(k) for k in (1, 2, 3)]
    for other in others:
        greet(other)

    rel_steps = n_rel // chunks.shape[1]

    def load(i):
        return pltpu.make_async_copy(
            chunk(relations, i, chunks.shape[1]), chunks.at[i % 2], chunk_sem.at[i % 2]
        )

    load(0).start()
    load(1).start()

    table[...] = entities[...]
    table_bf[...] = entities[...].astype(BF16)
    requests_2[...] = jnp.zeros_like(requests_2)
    for t in range(2):
        requests_2[t, shards, 0:1, :n_own] = neg_rows[t]

    def name_negatives(named):
        column = jnp.transpose(named[shards])[:n_own, 0:1]
        own_negs[...] = dot(hot(column, rows), table_bf[...]).astype(BF16)

    name_negatives(requests_2.at[0])
    pl.semaphore_wait(barrier, shards - 1 + len(others))

    def index_edges():
        for t in range(2):
            meta[t : t + 1, :] = dst_owner[t, 0]
            meta[2 + t : 3 + t, :] = src_row[t, 0]
            meta[4 + t : 5 + t, :] = rel_id[t, 0]
        meta[6:8, :] = jnp.zeros((2, edges), jnp.int32)
        meta_t[...] = jnp.transpose(meta[...])

    def plan(t):
        lower_tri = jnp.where(
            lax.broadcasted_iota(jnp.int32, (128, 128), 1)
            < lax.broadcasted_iota(jnp.int32, (128, 128), 0),
            1.0,
            0.0,
        ).astype(BF16)
        shard_rows = lax.broadcasted_iota(jnp.int32, (shards, 128), 0)
        base = jnp.zeros((1, 128), F32)
        upper = jnp.zeros((shards, LANES), F32)
        lower = jnp.zeros((shards, LANES), F32)
        for b in range(edges // 128):
            at = slice(b * 128, b * 128 + 128)
            owner = meta_t[at, t : t + 1]
            chosen = hot(owner, 128)
            chosen_f = chosen.astype(F32)
            count = dot(lower_tri, chosen) + base
            rank = jnp.sum(count * chosen_f, axis=1, keepdims=True).astype(jnp.int32)
            base = base + jnp.sum(chosen_f, axis=0, keepdims=True)
            meta_t[at, 6 + t : 7 + t] = owner * capacity + rank
            by_rank = hot(rank, LANES)
            row = dst_row[t, 0, :, at]
            named = meta[t : t + 1, at] == shard_rows
            part = lambda value: dot(jnp.where(named, value.astype(F32), 0.0).astype(BF16), by_rank)
            upper = upper + part(lax.shift_right_logical(row, 5))
            lower = lower + part(row & 31)
        asking = (upper * 32.0 + lower).astype(jnp.int32)
        for o in range(shards):
            requests_2[t, o, 0:1, :] = asking[o : o + 1, :]

    def request_copy(t, k):
        target = lax.rem(s + k, shards)
        return pltpu.make_async_remote_copy(
            src_ref=requests_2.at[t, target], dst_ref=asked_2.at[t, s],
            send_sem=req_send.at[t, k], recv_sem=req_recv.at[t, k],
            device_id=(g, target), device_id_type=MESH,
        )

    def ask(t):
        plan(t)
        each(1, shards, lambda k: request_copy(t, k).start())
        asked_2[t, s] = requests_2[t, s]
        asked_2[t, shards] = requests_2[t, shards]

    forward = pltpu.make_async_remote_copy(
        src_ref=asked_2.at[1], dst_ref=asked_next, send_sem=next_sem.at[0], recv_sem=next_sem.at[1],
        device_id=(next_g, s), device_id_type=MESH,
    )

    def look_relations(t):
        def step(i, carry):
            at = pl.ds(pl.multiple_of(i * tile, 128), tile)
            picked = hot(meta_t[at, :][:, 4 + t : 5 + t], n_rel)
            rel_rows_2[t, at, :] = dot(picked, high[...]) + dot(picked, low[...])
            return carry

        lax.fori_loop(0, 3, step, 0)

    def round_of(t):
        to_g = prev_g if t else g
        from_g = next_g if t else g
        first = 0 if t else 1
        negs, got, back = negs_2.at[t], got_2.at[t], back_2.at[t]
        pair_got, neg_got, rel_rows = pair_got_2.at[t], neg_got_2.at[t], rel_rows_2.at[t]
        wanted = asked_next if t else asked_2.at[0]
        limit = lengths[t, 0, 0]

        def live(i):
            place = lax.broadcasted_iota(jnp.int32, (tile, 1), 0) + i * tile
            return place < limit

        my_block = y_lo * depth + z

        def neg_copy(k):
            return pltpu.make_async_remote_copy(
                src_ref=own_negs, dst_ref=chunk(negs, my_block, n_own),
                send_sem=neg_sems.at[t, 0, k], recv_sem=neg_sems.at[t, 1, k],
                device_id=(to_g, along(k)), device_id_type=MESH,
            )

        neg_pair = pltpu.make_async_remote_copy(
            src_ref=chunk(negs, y_lo, n_side), dst_ref=chunk(negs, y_lo, n_side),
            send_sem=neg_sems.at[t, 0, depth], recv_sem=neg_sems.at[t, 1, depth],
            device_id=(g, pair_s), device_id_type=MESH,
        )

        def row_copy(k):
            target = lax.rem(s + k, shards)
            return pltpu.make_async_remote_copy(
                src_ref=chunk(sent, target, capacity), dst_ref=chunk(got, s, capacity),
                send_sem=row_send.at[t, k], recv_sem=row_recv.at[t, k],
                device_id=(to_g, target), device_id_type=MESH,
            )

        pair_copy = pltpu.make_async_remote_copy(
            src_ref=chunk(neg_send, 1 - y_lo, n_side), dst_ref=pair_got,
            send_sem=pair_sems.at[t, 0], recv_sem=pair_sems.at[t, 1],
            device_id=(g, pair_s), device_id_type=MESH,
        )

        def neg_grad_copy(k):
            return pltpu.make_async_remote_copy(
                src_ref=chunk(pair_sum, z_at(k), n_own), dst_ref=chunk(neg_got, z, n_own),
                send_sem=ngr_send.at[t, k], recv_sem=ngr_recv.at[t, k],
                device_id=(from_g, along(k)), device_id_type=MESH,
            )

        def query_copy(k):
            target = lax.rem(s + k, shards)
            return pltpu.make_async_remote_copy(
                src_ref=chunk(queries, target, capacity), dst_ref=chunk(back, s, capacity),
                send_sem=grad_send.at[t, k], recv_sem=grad_recv.at[t, k],
                device_id=(from_g, target), device_id_type=MESH,
            )

        if t:
            forward.wait()
            name_negatives(asked_next)
        else:
            negs[pl.ds(pl.multiple_of(my_block * n_own, 16), n_own), :] = own_negs[...]
        each(first, depth, lambda k: neg_copy(k).start())

        if t == 0:
            index_edges()
            ask(0)
            acc_t[...] = jnp.transpose(row_acc[...])
            for i in range(rel_steps):
                load(i).wait()
                value = chunks[i % 2]
                top = value.astype(BF16)
                at = slice(i * chunks.shape[1], (i + 1) * chunks.shape[1])
                high[at, :] = top
                low[at, :] = (value - top.astype(F32)).astype(BF16)
                if i + 2 < rel_steps:
                    load(i + 2).start()
            each(1, shards, lambda k: request_copy(0, k).wait())

        def answer(who):
            columns = jnp.transpose(wanted[who])[:capacity, :]
            asked_t[pl.ds(pl.multiple_of(who * capacity, 16), capacity), :] = columns
            return dot(hot(columns[:, 0:1], rows), table_bf[...]).astype(BF16)

        def send_rows(k):
            target = lax.rem(s + k, shards)
            sent[pl.ds(pl.multiple_of(target * capacity, 16), capacity), :] = answer(target)
            row_copy(k).start()

        each(first, shards, send_rows)
        if t == 0:
            own_block = pl.ds(pl.multiple_of(s * capacity, 16), capacity)
            sent[own_block, :] = answer(s)
            got[own_block, :] = sent[own_block, :]
        each(first, depth, lambda k: neg_copy(k).wait())
        neg_pair.start()

        if t == 0:
            look_relations(0)

        def look_sources(i, carry):
            at = pl.ds(pl.multiple_of(i * tile, 128), tile)
            emb = dot(hot(meta_t[at, :][:, 2 + t : 3 + t], rows), table_bf[...])
            src_emb[at, :] = emb.astype(BF16)
            query_bf[at, :] = jnp.where(live(i), emb * rel_rows[at, :], 0.0).astype(BF16)
            return carry

        lax.fori_loop(0, 3, look_sources, 0)

        neg_pair.wait()
        neg_acc[...] = jnp.zeros_like(neg_acc)

        def against_negatives(i, carry):
            at = pl.ds(pl.multiple_of(i * tile, 128), tile)
            query = query_bf[at, :]
            scores = lax.dot_general(
                query, negs[...], (((1,), (1,)), ((), ())), preferred_element_type=F32
            )
            weight = jnp.where(
                live(i), (jnp.tanh(scores * 0.5) + 1.0) * (0.5 / n_neg), 0.0
            ).astype(BF16)
            query_grad[at, :] = dot(weight, negs[...])
            neg_acc[...] += dot(jnp.transpose(query.astype(F32)).astype(BF16), weight)
            return carry

        lax.fori_loop(0, 3, against_negatives, 0)
        neg_send[...] = jnp.transpose(neg_acc[...]).astype(BF16)
        pair_copy.start()

        def mark_slots(i):
            at = pl.ds(pl.multiple_of(i * 128, 128), 128)
            by_slot[at, :] = hot(meta_t[at, :][:, 6 + t : 7 + t], slots)

        each(0, edges // 128, mark_slots)

        def mark_slots_t(i):
            at = pl.multiple_of(i * 128, 128)
            by_slot_t[pl.ds(at, 128), :] = hot_t(slot_row, 128, at)

        slot_row = jnp.transpose(meta_t[...])[6 + t : 7 + t, :]
        each(0, slots // 128, mark_slots_t)

        def query_block(target):
            at = pl.ds(pl.multiple_of(target * capacity, 16), capacity)
            return dot(by_slot_t[at, :], query_bf[...]).astype(BF16)

        def send_query(k):
            target = lax.rem(s + k, shards)
            queries[pl.ds(pl.multiple_of(target * capacity, 16), capacity), :] = query_block(target)
            row_copy(k).wait_send()
            query_copy(k).start()

        each(first, shards, send_query)
        if t == 0:
            back[own_block, :] = query_block(s)

        pair_copy.wait()
        mine_side = pl.ds(pl.multiple_of(y_lo * n_side, 16), n_side)
        pair_sum[...] = (neg_send[mine_side, :].astype(F32) + pair_got[...].astype(F32)).astype(BF16)
        if t == 0:
            own = pl.ds(pl.multiple_of(z * n_own, 16), n_own)
            neg_got[own, :] = pair_sum[own, :]
        each(first, depth, lambda k: neg_grad_copy(k).start())
        asked_rows = jnp.transpose(asked_t[...])[0:1, :]

        def mark_asked(i):
            at = pl.multiple_of(i * 128, 128)
            by_asked_t[pl.ds(at, 128), :] = hot_t(asked_rows, 128, at)

        each(0, rows // 128, mark_asked)
        if t == 0:
            ask(1)

        n_half, n_quarter = n_rel // 2, n_rel // 4
        mine, theirs = core * n_half, (1 - core) * n_half
        if t:

            def mark_relations(i):
                at = pl.multiple_of(i * 128, 128)
                by_rel_t[pl.ds(at, 128), :] = hot_t(meta[4 + t : 5 + t, :], 128, theirs + at)

            each(0, n_half // 128, mark_relations)

        each(first, shards, lambda k: row_copy(k).wait_recv())

        def positives(i, carry):
            at = pl.ds(pl.multiple_of(i * tile, 128), tile)
            emb = src_emb[at, :].astype(F32)
            rel = rel_rows[at, :]
            query = emb * rel
            dst = dot(by_slot[at, :], got[...])
            positive = jnp.sum(query * dst, axis=1, keepdims=True)
            weight = jnp.where(live(i), (jnp.tanh(positive * -0.5) + 1.0) * -0.5, 0.0)
            grad = weight * dst + query_grad[at, :]
            src_grad[at, :] = (grad * rel).astype(BF16)
            rel_grad[at, :] = (grad * emb).astype(BF16)
            return carry

        lax.fori_loop(0, 3, positives, 0)

        def scatter_sources():
            def step(i):
                at = pl.multiple_of(i * 256, 256)
                total[pl.ds(at, 256), :] = dot(hot_t(meta[2 + t : 3 + t, :], 256, at), src_grad[...])

            each(0, rows // 256, step)

        def take_grads():
            each(first, depth, lambda k: neg_grad_copy(k).wait())
            summed = neg_got[0:n_own, :].astype(F32)
            for k in range(1, depth):
                summed += neg_got[k * n_own : (k + 1) * n_own, :].astype(F32)
            upper = summed.astype(BF16)
            lower = (summed - upper.astype(F32)).astype(BF16)
            picked = hot_t(wanted[shards][0:1, :n_own], rows)
            total[...] += dot(picked, upper) + dot(picked, lower)

            def weigh(who):
                at = pl.ds(pl.multiple_of(who * capacity, 16), capacity)
                query = back[at, :].astype(F32)
                positive = jnp.sum(query * sent[at, :].astype(F32), axis=1, keepdims=True)
                weight = (jnp.tanh(positive * -0.5) + 1.0) * -0.5
                back[at, :] = (weight * query).astype(BF16)

            def take_one(k):
                query_copy(k).wait()
                weigh(lax.rem(s + shards - k, shards))

            if t == 0:
                weigh(s)
            each(first, shards, take_one)
            for i in range(rows // 128):
                at = slice(i * 128, i * 128 + 128)
                grad = total[at, :] + dot(by_asked_t[at, :], back[...])
                acc = acc_t[:, i : i + 1] + jnp.sum(grad * grad, axis=1, keepdims=True) * (1.0 / width)
                fresh = table[at, :] - LEARN_RATE * grad / jnp.sqrt(acc)
                acc_t[:, i : i + 1] = acc
                table[at, :] = fresh
                if t == 0:
                    table_bf[at, :] = fresh.astype(BF16)

        if t == 0:
            scatter_sources()

            def scatter(i):
                at = pl.multiple_of(i * 512, 512)
                part = dot(hot_t(meta[4:5, :], 512, at), rel_grad[...])
                half[pl.ds(at, 512), :] = part.astype(BF16)

            each(0, n_rel // 512, scatter)
            look_relations(1)
            each(1, shards, lambda k: request_copy(1, k).wait())
            forward.start()
            take_grads()
            return

        big, small, least = n_quarter // 4, n_quarter // 16, n_rel // 256

        def rel_copy(src, dst, sem, where):
            return pltpu.make_async_remote_copy(
                src_ref=src, dst_ref=dst, send_sem=rel_send.at[sem], recv_sem=rel_recv.at[sem],
                device_id=where, device_id_type=MESH,
            )

        def run(copies):
            for copy in copies:
                copy.start()
            return copies

        def finish(copies):
            for copy in copies:
                copy.wait()

        def scatter_theirs(i):
            at = pl.multiple_of(i * 512, 512)
            where = pl.ds(pl.multiple_of(theirs + at, 512), 512)
            part = dot(by_rel_t[pl.ds(at, 512), :], rel_grad[...])
            half[where, :] = (half[where, :].astype(F32) + part).astype(BF16)

        def scatter_mine(i):
            at = pl.multiple_of(mine + i * 512, 512)
            part = dot(hot_t(meta[5:6, :], 512, at), rel_grad[...])
            half[pl.ds(at, 512), :] = (half[pl.ds(at, 512), :].astype(F32) + part).astype(BF16)

        each(0, n_half // 512, scatter_theirs)
        copies = run([rel_copy(span(half, theirs, n_half), rel_got_c, 0, core_dev)])
        each(0, n_half // 512, scatter_mine)
        finish(copies)

        def add_core(i):
            at = pl.multiple_of(i * 256, 256)
            mine_at = pl.ds(pl.multiple_of(mine + at, 256), 256)
            value = half[mine_at, :].astype(F32) + rel_got_c[pl.ds(at, 256), :].astype(F32)
            rel_got_c[pl.ds(at, 256), :] = value.astype(BF16)

        each(0, n_half // 256, add_core)
        chip = rel_got_c
        copies = run(
            [rel_copy(span(chip, x_at(k) * big, big), got_x.at[k - 1], k, x_dev(k)) for k in (1, 2, 3)]
            + [
                rel_copy(span(chip, n_quarter + y_at(k) * big, big), got_y.at[k - 1], 3 + k, y_dev(k))
                for k in (1, 2, 3)
            ]
        )
        scatter_sources()
        finish(copies)

        def sum_of(ref, at, size, arrived):
            value = ref[pl.ds(pl.multiple_of(at, 16), size), :].astype(F32)
            for k in range(arrived.shape[0]):
                value += arrived[k].astype(F32)
            return value.astype(BF16)

        sum_x[...] = sum_of(chip, x * big, big, got_x)
        sum_y[...] = sum_of(chip, n_quarter + y * big, big, got_y)
        copies = run(
            [rel_copy(span(sum_x, y_at(k) * small, small), got_y2.at[k - 1], 6 + k, y_dev(k)) for k in (1, 2, 3)]
            + [rel_copy(span(sum_y, x_at(k) * small, small), got_x2.at[k - 1], 9 + k, x_dev(k)) for k in (1, 2, 3)]
        )
        finish(copies)
        last[0:small, :] = sum_of(sum_x, y * small, small, got_y2)
        last[small : 2 * small, :] = sum_of(sum_y, x * small, small, got_x2)
        copies = run(
            [rel_copy(span(last, z_at(k) * least, least), got_z.at[k - 1], 12 + k, z_dev(k)) for k in range(1, 8)]
        )
        finish(copies)
        side = z // 4
        at_x = mine + x * big + y * small
        at_y = mine + n_quarter + y * big + x * small
        at_z = at_x + side * (at_y - at_x) + lax.rem(z, 4) * least
        rel_out[pl.ds(pl.multiple_of(at_z, 16), least), :] = sum_of(last, z * least, least, got_z)
        same = lambda at, size: [span(rel_out, at, size)] * 2
        finish(run([rel_copy(*same(at_z, least), 19 + k, z_dev(k)) for k in range(1, 8)]))
        finish(
            run(
                [rel_copy(*same(at_x, small), 26 + k, y_dev(k)) for k in (1, 2, 3)]
                + [rel_copy(*same(at_y, small), 29 + k, x_dev(k)) for k in (1, 2, 3)]
            )
        )
        copies = run(
            [rel_copy(*same(mine + x * big, big), 32 + k, x_dev(k)) for k in (1, 2, 3)]
            + [rel_copy(*same(mine + n_quarter + y * big, big), 35 + k, y_dev(k)) for k in (1, 2, 3)]
        )
        take_grads()
        finish(copies)
        finish(run([rel_copy(*same(mine, n_half), 39, core_dev)]))

    round_of(0)
    round_of(1)
    acc_out[...] = jnp.transpose(acc_t[...])


def train(entities, row_acc, relations, src_row, rel_id, dst_owner, dst_row, neg_rows, lengths):
    groups, shards = lax.axis_size("grp"), lax.axis_size("shard")
    rows, width = entities.shape
    n_rel, edges, n_own = relations.shape[0], src_row.shape[-1], neg_rows.shape[-1]
    capacity = 2 * edges // shards
    n_neg, slots, depth = shards * n_own, shards * capacity, shards // 2
    bf = lambda *shape: pltpu.VMEM(shape + (width,), BF16)
    f32 = lambda *shape: pltpu.VMEM(shape + (width,), F32)
    i32 = lambda *shape: pltpu.VMEM(shape, jnp.int32)
    sems = lambda *shape: pltpu.SemaphoreType.DMA(shape)
    scratch = [
        i32(8, edges), i32(edges, 8),
        i32(2, shards + 1, 8, LANES), i32(2, shards + 1, 8, LANES), i32(shards + 1, 8, LANES), i32(slots, 8),
        f32(2, 512), bf(n_rel), bf(n_rel), bf(rows), pltpu.VMEM((rows // 8, 8), F32),
        bf(n_own), bf(2, n_neg), bf(slots), bf(slots), bf(2, slots), bf(2, slots),
        bf(n_neg), bf(2, n_neg // 2), bf(n_neg // 2), bf(2, n_neg // 2),
        bf(edges), f32(2, edges), bf(edges), f32(edges), bf(edges), bf(edges),
        pltpu.VMEM((width, n_neg), F32), f32(rows),
        pltpu.VMEM((edges, slots), BF16), pltpu.VMEM((slots, edges), BF16),
        pltpu.VMEM((rows, slots), BF16), pltpu.VMEM((n_rel // 2, edges), BF16),
        bf(n_rel), bf(n_rel // 2),
        bf(3, n_rel // 16), bf(3, n_rel // 16), bf(n_rel // 16), bf(n_rel // 16),
        bf(3, n_rel // 64), bf(3, n_rel // 64), bf(n_rel // 32), bf(7, n_rel // 256),
        sems(2), sems(2, shards), sems(2, shards), sems(2, 2, depth + 1),
        sems(2, shards), sems(2, shards), sems(2, 2),
        sems(2, depth), sems(2, depth), sems(2, shards), sems(2, shards),
        sems(2), sems(40), sems(40),
    ]
    vmem = pl.BlockSpec(memory_space=pltpu.VMEM)
    return pl.pallas_call(
        functools.partial(train_kernel, groups, shards, edges, capacity, n_own),
        out_shape=[
            jax.ShapeDtypeStruct((rows, width), F32),
            jax.ShapeDtypeStruct((8, rows // 8), F32),
            jax.ShapeDtypeStruct((n_rel, width), BF16),
        ],
        in_specs=[vmem, vmem, pl.BlockSpec(memory_space=pl.ANY)] + [vmem] * 5
        + [pl.BlockSpec(memory_space=pltpu.SMEM)],
        out_specs=[vmem] * 3,
        scratch_shapes=scratch,
        compiler_params=pltpu.CompilerParams(
            collective_id=0, has_side_effects=True, vmem_limit_bytes=60 << 20
        ),
        name="train",
    )(
        entities, row_acc.reshape(8, rows // 8), relations, src_row, rel_id,
        dst_owner[..., 0], dst_row, neg_rows, lengths,
    )


def per_device(
    entities, row_acc, relations, rel_acc, src_row, rel_id, dst_owner, dst_row, neg_rows, lengths
):
    table, accum, rel_total = train(
        entities, row_acc, relations, src_row, rel_id, dst_owner, dst_row, neg_rows, lengths
    )
    new_rel, new_racc = adagrad(relations, rel_acc, rel_total.astype(F32))
    return (table, accum.reshape(-1), new_rel, new_racc)


def solution(mesh):
    in_specs = (
        P(("grp", "shard"), None),
        P(("grp", "shard")),
        P(),
        P(),
        P(None, "grp", "shard", None),
        P(None, "grp", "shard", None),
        P(None, "grp", "shard", None, None),
        P(None, "grp", "shard", None),
        P(None, "grp", "shard"),
        P(None, "grp", "shard"),
    )
    out_specs = (P(("grp", "shard"), None), P(("grp", "shard")), P(), P())
    return jax.shard_map(
        per_device, mesh=mesh, in_specs=in_specs, out_specs=out_specs, check_vma=False
    )
```

```python
import functools
import jax
import jax.numpy as jnp
from jax import lax
from jax.experimental import pallas as pl
from jax.experimental.pallas import tpu as pltpu
from jax.sharding import PartitionSpec as P

LEARN_RATE = 0.3
MESH = pl.DeviceIdType.MESH
F32 = jnp.float32
BF16 = jnp.bfloat16
LANES = 256


def adagrad(table, accum, gradient):
    total = accum + jnp.mean(gradient * gradient, axis=-1)
    return (table - LEARN_RATE * gradient / jnp.sqrt(total)[..., None], total)


def dot(a, b):
    return jnp.dot(a, b, preferred_element_type=F32)


def hot(index, size):
    places = lax.broadcasted_iota(jnp.int32, (index.shape[0], size), 1)
    return jnp.where(places == index, 1.0, 0.0).astype(BF16)


def hot_t(index, size, first=0):
    places = lax.broadcasted_iota(jnp.int32, (size, index.shape[1]), 0) + first
    return jnp.where(places == index, 1.0, 0.0).astype(BF16)


def train_kernel(groups, shards, edges, capacity, n_own, *refs):
    (entities, row_acc, relations, src_row, rel_id, dst_owner, dst_row, neg_rows, lengths,
     table, acc_out, rel_out,
     meta, meta_t, requests_2, asked_2, asked_next, asked_t, chunks, high, low, table_bf, acc_t,
     own_negs, negs_2, sent, queries, got_2, back_2, neg_send, pair_got_2, pair_sum, neg_got_2,
     src_emb, rel_rows_2, query_bf, query_grad, src_grad, rel_grad, neg_acc, total,
     by_slot, by_slot_t, by_asked_t, by_rel_t,
     half, rel_got_c, got_x, got_y, sum_x, sum_y, got_x2, got_y2, last, got_z,
     chunk_sem, req_send, req_recv, neg_sems, row_send, row_recv, pair_sems,
     ngr_send, ngr_recv, grad_send, grad_recv, next_sem, rel_send, rel_recv) = refs

    rows, width = table.shape
    n_rel = relations.shape[0]
    n_neg = shards * n_own
    n_side = n_neg // 2
    depth = shards // 2
    slots = shards * capacity
    g, s = lax.axis_index("grp"), lax.axis_index("shard")
    next_g, prev_g = lax.rem(g + 1, groups), lax.rem(g + groups - 1, groups)
    tile = edges // 3
    chunk = lambda ref, i, size: ref.at[pl.ds(pl.multiple_of(i * size, 16), size)]
    span = lambda ref, at, size: ref.at[pl.ds(pl.multiple_of(at, 16), size)]

    x, y_hi, core = g // 4, lax.rem(g // 2, 2), lax.rem(g, 2)
    z, y_lo = s // 2, lax.rem(s, 2)
    y = y_hi * 2 + y_lo
    pair_s = z * 2 + 1 - y_lo
    along = lambda k: lax.rem(z + k, depth) * 2 + y_lo

    def device(x, y, z, core):
        return (x * 4 + (y // 2) * 2 + core, z * 2 + lax.rem(y, 2))

    x_at = lambda k: lax.rem(x + k, 4)
    y_at = lambda k: lax.rem(y + k, 4)
    z_at = lambda k: lax.rem(z + k, 8)
    x_dev = lambda k: device(x_at(k), y, z, core)
    y_dev = lambda k: device(x, y_at(k), z, core)
    z_dev = lambda k: device(x, y, z_at(k), core)
    core_dev = device(x, y, z, 1 - core)

    def each(begin, end, body):
        def step(k, carry):
            body(k)
            return carry

        lax.fori_loop(begin, end, step, 0)

    barrier = pltpu.get_barrier_semaphore()

    def greet(where):
        pl.semaphore_signal(barrier, inc=1, device_id=where, device_id_type=MESH)

    each(1, shards, lambda k: greet((g, lax.rem(s + shards - k, shards))))
    others = [(prev_g, s), core_dev] + [x_dev(k) for k in (1, 2, 3)] + [y_dev(k) for k in (1, 2, 3)]
    for other in others:
        greet(other)

    rel_steps = n_rel // chunks.shape[1]

    def load(i):
        return pltpu.make_async_copy(
            chunk(relations, i, chunks.shape[1]), chunks.at[i % 2], chunk_sem.at[i % 2]
        )

    load(0).start()
    load(1).start()

    table[...] = entities[...]
    table_bf[...] = entities[...].astype(BF16)
    requests_2[...] = jnp.zeros_like(requests_2)
    for t in range(2):
        requests_2[t, shards, 0:1, :n_own] = neg_rows[t]

    def name_negatives(named):
        column = jnp.transpose(named[shards])[:n_own, 0:1]
        own_negs[...] = dot(hot(column, rows), table_bf[...]).astype(BF16)

    name_negatives(requests_2.at[0])
    def index_edges():
        for t in range(2):
            meta[t : t + 1, :] = dst_owner[t, 0]
            meta[2 + t : 3 + t, :] = src_row[t, 0]
            meta[4 + t : 5 + t, :] = rel_id[t, 0]
        meta[6:8, :] = jnp.zeros((2, edges), jnp.int32)
        meta_t[...] = jnp.transpose(meta[...])

    def plan(t):
        lower_tri = jnp.where(
            lax.broadcasted_iota(jnp.int32, (128, 128), 1)
            < lax.broadcasted_iota(jnp.int32, (128, 128), 0),
            1.0,
            0.0,
        ).astype(BF16)
        shard_rows = lax.broadcasted_iota(jnp.int32, (shards, 128), 0)
        base = jnp.zeros((1, 128), F32)
        upper = jnp.zeros((shards, LANES), F32)
        lower = jnp.zeros((shards, LANES), F32)
        for b in range(edges // 128):
            at = slice(b * 128, b * 128 + 128)
            owner = meta_t[at, t : t + 1]
            chosen = hot(owner, 128)
            chosen_f = chosen.astype(F32)
            count = dot(lower_tri, chosen) + base
            rank = jnp.sum(count * chosen_f, axis=1, keepdims=True).astype(jnp.int32)
            base = base + jnp.sum(chosen_f, axis=0, keepdims=True)
            meta_t[at, 6 + t : 7 + t] = owner * capacity + rank
            by_rank = hot(rank, LANES)
            row = dst_row[t, 0, :, at]
            named = meta[t : t + 1, at] == shard_rows
            part = lambda value: dot(jnp.where(named, value.astype(F32), 0.0).astype(BF16), by_rank)
            upper = upper + part(lax.shift_right_logical(row, 5))
            lower = lower + part(row & 31)
        asking = (upper * 32.0 + lower).astype(jnp.int32)
        for o in range(shards):
            requests_2[t, o, 0:1, :] = asking[o : o + 1, :]

    def request_copy(t, k):
        target = lax.rem(s + k, shards)
        return pltpu.make_async_remote_copy(
            src_ref=requests_2.at[t, target], dst_ref=asked_2.at[t, s],
            send_sem=req_send.at[t, k], recv_sem=req_recv.at[t, k],
            device_id=(g, target), device_id_type=MESH,
        )

    def ask(t):
        each(1, shards, lambda k: request_copy(t, k).start())
        asked_2[t, s] = requests_2[t, s]
        asked_2[t, shards] = requests_2[t, shards]

    index_edges()
    plan(0)
    pl.semaphore_wait(barrier, shards - 1 + len(others))

    forward = pltpu.make_async_remote_copy(
        src_ref=asked_2.at[1], dst_ref=asked_next, send_sem=next_sem.at[0], recv_sem=next_sem.at[1],
        device_id=(next_g, s), device_id_type=MESH,
    )

    def look_relations(t):
        def step(i, carry):
            at = pl.ds(pl.multiple_of(i * tile, 128), tile)
            picked = hot(meta_t[at, :][:, 4 + t : 5 + t], n_rel)
            rel_rows_2[t, at, :] = dot(picked, high[...]) + dot(picked, low[...])
            return carry

        lax.fori_loop(0, 3, step, 0)

    def round_of(t):
        to_g = prev_g if t else g
        from_g = next_g if t else g
        first = 0 if t else 1
        negs, got, back = negs_2.at[t], got_2.at[t], back_2.at[t]
        pair_got, neg_got, rel_rows = pair_got_2.at[t], neg_got_2.at[t], rel_rows_2.at[t]
        wanted = asked_next if t else asked_2.at[0]
        limit = lengths[0:1, t : t + 1]

        def live(i):
            place = lax.broadcasted_iota(jnp.int32, (tile, 1), 0) + i * tile
            return place < limit

        my_block = y_lo * depth + z

        def neg_copy(k):
            return pltpu.make_async_remote_copy(
                src_ref=own_negs, dst_ref=chunk(negs, my_block, n_own),
                send_sem=neg_sems.at[t, 0, k], recv_sem=neg_sems.at[t, 1, k],
                device_id=(to_g, along(k)), device_id_type=MESH,
            )

        neg_pair = pltpu.make_async_remote_copy(
            src_ref=chunk(negs, y_lo, n_side), dst_ref=chunk(negs, y_lo, n_side),
            send_sem=neg_sems.at[t, 0, depth], recv_sem=neg_sems.at[t, 1, depth],
            device_id=(g, pair_s), device_id_type=MESH,
        )

        def row_copy(k):
            target = lax.rem(s + k, shards)
            return pltpu.make_async_remote_copy(
                src_ref=chunk(sent, target, capacity), dst_ref=chunk(got, s, capacity),
                send_sem=row_send.at[t, k], recv_sem=row_recv.at[t, k],
                device_id=(to_g, target), device_id_type=MESH,
            )

        pair_copy = pltpu.make_async_remote_copy(
            src_ref=chunk(neg_send, 1 - y_lo, n_side), dst_ref=pair_got,
            send_sem=pair_sems.at[t, 0], recv_sem=pair_sems.at[t, 1],
            device_id=(g, pair_s), device_id_type=MESH,
        )

        def neg_grad_copy(k):
            return pltpu.make_async_remote_copy(
                src_ref=chunk(pair_sum, z_at(k), n_own), dst_ref=chunk(neg_got, z, n_own),
                send_sem=ngr_send.at[t, k], recv_sem=ngr_recv.at[t, k],
                device_id=(from_g, along(k)), device_id_type=MESH,
            )

        def query_copy(k):
            target = lax.rem(s + k, shards)
            return pltpu.make_async_remote_copy(
                src_ref=chunk(queries, target, capacity), dst_ref=chunk(back, s, capacity),
                send_sem=grad_send.at[t, k], recv_sem=grad_recv.at[t, k],
                device_id=(from_g, target), device_id_type=MESH,
            )

        if t:
            forward.wait()
            name_negatives(asked_next)
        else:
            ask(0)
            negs[pl.ds(pl.multiple_of(my_block * n_own, 16), n_own), :] = own_negs[...]
        each(first, depth, lambda k: neg_copy(k).start())

        if t == 0:
            acc_t[...] = jnp.transpose(row_acc[...])
            for i in range(rel_steps):
                load(i).wait()
                value = chunks[i % 2]
                top = value.astype(BF16)
                at = slice(i * chunks.shape[1], (i + 1) * chunks.shape[1])
                high[at, :] = top
                low[at, :] = (value - top.astype(F32)).astype(BF16)
                if i + 2 < rel_steps:
                    load(i + 2).start()
            each(1, shards, lambda k: request_copy(0, k).wait())

        def answer(who):
            columns = jnp.transpose(wanted[who])[:capacity, :]
            asked_t[pl.ds(pl.multiple_of(who * capacity, 16), capacity), :] = columns
            return dot(hot(columns[:, 0:1], rows), table_bf[...]).astype(BF16)

        def send_rows(k):
            target = lax.rem(s + k, shards)
            sent[pl.ds(pl.multiple_of(target * capacity, 16), capacity), :] = answer(target)
            row_copy(k).start()

        each(first, shards, send_rows)
        if t == 0:
            own_block = pl.ds(pl.multiple_of(s * capacity, 16), capacity)
            sent[own_block, :] = answer(s)
            got[own_block, :] = sent[own_block, :]
        each(first, depth, lambda k: neg_copy(k).wait())
        neg_pair.start()

        if t == 0:
            look_relations(0)

        def look_sources(i, carry):
            at = pl.ds(pl.multiple_of(i * tile, 128), tile)
            emb = dot(hot(meta_t[at, :][:, 2 + t : 3 + t], rows), table_bf[...])
            src_emb[at, :] = emb.astype(BF16)
            query_bf[at, :] = jnp.where(live(i), emb * rel_rows[at, :], 0.0).astype(BF16)
            return carry

        lax.fori_loop(0, 3, look_sources, 0)

        neg_pair.wait()
        neg_acc[...] = jnp.zeros_like(neg_acc)

        def against_negatives(i, carry):
            at = pl.ds(pl.multiple_of(i * tile, 128), tile)
            query = query_bf[at, :]
            scores = lax.dot_general(
                query, negs[...], (((1,), (1,)), ((), ())), preferred_element_type=F32
            )
            weight = jnp.where(
                live(i), (jnp.tanh(scores * 0.5) + 1.0) * (0.5 / n_neg), 0.0
            ).astype(BF16)
            query_grad[at, :] = dot(weight, negs[...])
            neg_acc[...] += dot(jnp.transpose(query.astype(F32)).astype(BF16), weight)
            return carry

        lax.fori_loop(0, 3, against_negatives, 0)
        neg_send[...] = jnp.transpose(neg_acc[...]).astype(BF16)
        pair_copy.start()

        def mark_slots(i):
            at = pl.ds(pl.multiple_of(i * 128, 128), 128)
            by_slot[at, :] = hot(meta_t[at, :][:, 6 + t : 7 + t], slots)

        each(0, edges // 128, mark_slots)

        def mark_slots_t(i):
            at = pl.multiple_of(i * 128, 128)
            by_slot_t[pl.ds(at, 128), :] = hot_t(slot_row, 128, at)

        slot_row = jnp.transpose(meta_t[...])[6 + t : 7 + t, :]
        each(0, slots // 128, mark_slots_t)

        asked_rows = jnp.transpose(asked_t[...])[0:1, :]

        def mark_asked(i):
            at = pl.multiple_of(i * 128, 128)
            by_asked_t[pl.ds(at, 128), :] = hot_t(asked_rows, 128, at)

        each(0, rows // 128, mark_asked)

        n_half, n_quarter = n_rel // 2, n_rel // 4
        mine, theirs = core * n_half, (1 - core) * n_half
        if t:

            def mark_relations(i):
                at = pl.multiple_of(i * 128, 128)
                by_rel_t[pl.ds(at, 128), :] = hot_t(meta[4 + t : 5 + t, :], 128, theirs + at)

            each(0, n_half // 128, mark_relations)

        def query_block(target):
            at = pl.ds(pl.multiple_of(target * capacity, 16), capacity)
            return dot(by_slot_t[at, :], query_bf[...]).astype(BF16)

        def send_query(k):
            target = lax.rem(s + k, shards)
            queries[pl.ds(pl.multiple_of(target * capacity, 16), capacity), :] = query_block(target)
            row_copy(k).wait_send()
            query_copy(k).start()

        each(first, shards, send_query)
        if t == 0:
            back[own_block, :] = query_block(s)

        pair_copy.wait()
        mine_side = pl.ds(pl.multiple_of(y_lo * n_side, 16), n_side)
        pair_sum[...] = (neg_send[mine_side, :].astype(F32) + pair_got[...].astype(F32)).astype(BF16)
        if t == 0:
            own = pl.ds(pl.multiple_of(z * n_own, 16), n_own)
            neg_got[own, :] = pair_sum[own, :]
        if t == 0:
            each(1, depth, lambda k: neg_grad_copy(k).start())
        if t == 0:
            plan(1)
            ask(1)

        each(first, shards, lambda k: row_copy(k).wait_recv())

        def send_held():
            each(0, depth, lambda k: neg_grad_copy(k).start())

        def positives(i, carry):
            at = pl.ds(pl.multiple_of(i * tile, 128), tile)
            emb = src_emb[at, :].astype(F32)
            rel = rel_rows[at, :]
            query = emb * rel
            dst = dot(by_slot[at, :], got[...])
            positive = jnp.sum(query * dst, axis=1, keepdims=True)
            weight = jnp.where(live(i), (jnp.tanh(positive * -0.5) + 1.0) * -0.5, 0.0)
            grad = weight * dst + query_grad[at, :]
            src_grad[at, :] = (grad * rel).astype(BF16)
            rel_grad[at, :] = (grad * emb).astype(BF16)
            return carry

        lax.fori_loop(0, 3, positives, 0)

        def scatter_sources():
            def step(i):
                at = pl.multiple_of(i * 256, 256)
                total[pl.ds(at, 256), :] = dot(hot_t(meta[2 + t : 3 + t, :], 256, at), src_grad[...])

            each(0, rows // 256, step)

        def take_queries():
            each(first, shards, lambda k: query_copy(k).wait())

            def weigh(i):
                at = pl.ds(pl.multiple_of(i * 384, 128), 384)
                query = back[at, :].astype(F32)
                positive = jnp.sum(query * sent[at, :].astype(F32), axis=1, keepdims=True)
                weight = (jnp.tanh(positive * -0.5) + 1.0) * -0.5
                back[at, :] = (weight * query).astype(BF16)

            each(0, slots // 384, weigh)

            def add(i):
                at = pl.ds(pl.multiple_of(i * 256, 256), 256)
                total[at, :] += dot(by_asked_t[at, :], back[...])

            each(0, rows // 256, add)

        def take_negatives():
            each(first, depth, lambda k: neg_grad_copy(k).wait())
            summed = neg_got[0:n_own, :].astype(F32)
            for k in range(1, depth):
                summed += neg_got[k * n_own : (k + 1) * n_own, :].astype(F32)
            upper = summed.astype(BF16)
            lower = (summed - upper.astype(F32)).astype(BF16)
            named = wanted[shards][0:1, :n_own]
            for i in range(rows // 128):
                at = slice(i * 128, i * 128 + 128)
                picked = hot_t(named, 128, i * 128)
                grad = total[at, :] + dot(picked, upper) + dot(picked, lower)
                acc = acc_t[:, i : i + 1] + jnp.sum(grad * grad, axis=1, keepdims=True) * (1.0 / width)
                fresh = table[at, :] - LEARN_RATE * grad / jnp.sqrt(acc)
                acc_t[:, i : i + 1] = acc
                table[at, :] = fresh
                if t == 0:
                    table_bf[at, :] = fresh.astype(BF16)

        if t == 0:
            scatter_sources()

            def scatter(i):
                at = pl.multiple_of(i * 512, 512)
                part = dot(hot_t(meta[4:5, :], 512, at), rel_grad[...])
                half[pl.ds(at, 512), :] = part.astype(BF16)

            each(0, n_rel // 512, scatter)
            look_relations(1)
            each(1, shards, lambda k: request_copy(1, k).wait())
            forward.start()
            take_queries()
            take_negatives()
            return

        big, small, least = n_quarter // 4, n_quarter // 16, n_rel // 256

        def rel_copy(src, dst, sem, where):
            return pltpu.make_async_remote_copy(
                src_ref=src, dst_ref=dst, send_sem=rel_send.at[sem], recv_sem=rel_recv.at[sem],
                device_id=where, device_id_type=MESH,
            )

        def run(copies):
            for copy in copies:
                copy.start()
            return copies

        def finish(copies):
            for copy in copies:
                copy.wait()

        def scatter_theirs(i):
            at = pl.multiple_of(i * 512, 512)
            where = pl.ds(pl.multiple_of(theirs + at, 512), 512)
            part = dot(by_rel_t[pl.ds(at, 512), :], rel_grad[...])
            half[where, :] = (half[where, :].astype(F32) + part).astype(BF16)

        def scatter_mine(i):
            at = pl.multiple_of(mine + i * 512, 512)
            part = dot(hot_t(meta[5:6, :], 512, at), rel_grad[...])
            half[pl.ds(at, 512), :] = (half[pl.ds(at, 512), :].astype(F32) + part).astype(BF16)

        copies = []
        for i in range(2):
            each(i * (n_half // 1024), (i + 1) * (n_half // 1024), scatter_theirs)
            copies += run(
                [
                    rel_copy(
                        span(half, theirs + i * n_quarter, n_quarter),
                        span(rel_got_c, i * n_quarter, n_quarter), 40 * i, core_dev,
                    )
                ]
            )
        each(0, n_half // 512, scatter_mine)
        finish(copies)

        def add_core(i):
            at = pl.multiple_of(i * 256, 256)
            mine_at = pl.ds(pl.multiple_of(mine + at, 256), 256)
            value = half[mine_at, :].astype(F32) + rel_got_c[pl.ds(at, 256), :].astype(F32)
            rel_got_c[pl.ds(at, 256), :] = value.astype(BF16)

        each(0, n_half // 256, add_core)
        chip = rel_got_c
        copies = run(
            [rel_copy(span(chip, x_at(k) * big, big), got_x.at[k - 1], k, x_dev(k)) for k in (1, 2, 3)]
            + [
                rel_copy(span(chip, n_quarter + y_at(k) * big, big), got_y.at[k - 1], 3 + k, y_dev(k))
                for k in (1, 2, 3)
            ]
        )
        scatter_sources()
        finish(copies)

        def sum_of(ref, at, size, arrived):
            value = ref[pl.ds(pl.multiple_of(at, 16), size), :].astype(F32)
            for k in range(arrived.shape[0]):
                value += arrived[k].astype(F32)
            return value.astype(BF16)

        sum_x[...] = sum_of(chip, x * big, big, got_x)
        sum_y[...] = sum_of(chip, n_quarter + y * big, big, got_y)
        copies = run(
            [rel_copy(span(sum_x, y_at(k) * small, small), got_y2.at[k - 1], 6 + k, y_dev(k)) for k in (1, 2, 3)]
            + [rel_copy(span(sum_y, x_at(k) * small, small), got_x2.at[k - 1], 9 + k, x_dev(k)) for k in (1, 2, 3)]
        )
        finish(copies)
        last[0:small, :] = sum_of(sum_x, y * small, small, got_y2)
        last[small : 2 * small, :] = sum_of(sum_y, x * small, small, got_x2)
        copies = run(
            [rel_copy(span(last, z_at(k) * least, least), got_z.at[k - 1], 12 + k, z_dev(k)) for k in range(1, 8)]
        )
        finish(copies)
        side = z // 4
        at_x = mine + x * big + y * small
        at_y = mine + n_quarter + y * big + x * small
        at_z = at_x + side * (at_y - at_x) + lax.rem(z, 4) * least
        rel_out[pl.ds(pl.multiple_of(at_z, 16), least), :] = sum_of(last, z * least, least, got_z)
        same = lambda at, size: [span(rel_out, at, size)] * 2
        finish(run([rel_copy(*same(at_z, least), 19 + k, z_dev(k)) for k in range(1, 8)]))
        copies = run(
            [rel_copy(*same(at_x, small), 26 + k, y_dev(k)) for k in (1, 2, 3)]
            + [rel_copy(*same(at_y, small), 29 + k, x_dev(k)) for k in (1, 2, 3)]
        )
        send_held()
        finish(copies)
        copies = run(
            [rel_copy(*same(mine + x * big, big), 32 + k, x_dev(k)) for k in (1, 2, 3)]
            + [rel_copy(*same(mine + n_quarter + y * big, big), 35 + k, y_dev(k)) for k in (1, 2, 3)]
        )
        take_queries()
        finish(copies)
        copies = run([rel_copy(*same(mine, n_half), 39, core_dev)])
        take_negatives()
        finish(copies)

    round_of(0)
    round_of(1)
    acc_out[...] = jnp.transpose(acc_t[...])


def train(entities, row_acc, relations, src_row, rel_id, dst_owner, dst_row, neg_rows, lengths):
    groups, shards = lax.axis_size("grp"), lax.axis_size("shard")
    rows, width = entities.shape
    n_rel, edges, n_own = relations.shape[0], src_row.shape[-1], neg_rows.shape[-1]
    capacity = 2 * edges // shards
    n_neg, slots, depth = shards * n_own, shards * capacity, shards // 2
    bf = lambda *shape: pltpu.VMEM(shape + (width,), BF16)
    f32 = lambda *shape: pltpu.VMEM(shape + (width,), F32)
    i32 = lambda *shape: pltpu.VMEM(shape, jnp.int32)
    sems = lambda *shape: pltpu.SemaphoreType.DMA(shape)
    scratch = [
        i32(8, edges), i32(edges, 8),
        i32(2, shards + 1, 8, LANES), i32(2, shards + 1, 8, LANES), i32(shards + 1, 8, LANES), i32(slots, 8),
        f32(2, 512), bf(n_rel), bf(n_rel), bf(rows), pltpu.VMEM((rows // 8, 8), F32),
        bf(n_own), bf(2, n_neg), bf(slots), bf(slots), bf(2, slots), bf(2, slots),
        bf(n_neg), bf(2, n_neg // 2), bf(n_neg // 2), bf(2, n_neg // 2),
        bf(edges), f32(2, edges), bf(edges), f32(edges), bf(edges), bf(edges),
        pltpu.VMEM((width, n_neg), F32), f32(rows),
        pltpu.VMEM((edges, slots), BF16), pltpu.VMEM((slots, edges), BF16),
        pltpu.VMEM((rows, slots), BF16), pltpu.VMEM((n_rel // 2, edges), BF16),
        bf(n_rel), bf(n_rel // 2),
        bf(3, n_rel // 16), bf(3, n_rel // 16), bf(n_rel // 16), bf(n_rel // 16),
        bf(3, n_rel // 64), bf(3, n_rel // 64), bf(n_rel // 32), bf(7, n_rel // 256),
        sems(2), sems(2, shards), sems(2, shards), sems(2, 2, depth + 1),
        sems(2, shards), sems(2, shards), sems(2, 2),
        sems(2, depth), sems(2, depth), sems(2, shards), sems(2, shards),
        sems(2), sems(41), sems(41),
    ]
    vmem = pl.BlockSpec(memory_space=pltpu.VMEM)
    return pl.pallas_call(
        functools.partial(train_kernel, groups, shards, edges, capacity, n_own),
        out_shape=[
            jax.ShapeDtypeStruct((rows, width), F32),
            jax.ShapeDtypeStruct((8, rows // 8), F32),
            jax.ShapeDtypeStruct((n_rel, width), BF16),
        ],
        in_specs=[vmem, vmem, pl.BlockSpec(memory_space=pl.ANY)] + [vmem] * 6,
        out_specs=[vmem] * 3,
        scratch_shapes=scratch,
        compiler_params=pltpu.CompilerParams(
            collective_id=0, has_side_effects=True, vmem_limit_bytes=56 << 20
        ),
        name="train",
    )(
        entities, row_acc.reshape(8, rows // 8), relations, src_row, rel_id,
        dst_owner[..., 0], dst_row, neg_rows, lengths.reshape(1, 2),
    )


def per_device(
    entities, row_acc, relations, rel_acc, src_row, rel_id, dst_owner, dst_row, neg_rows, lengths
):
    table, accum, rel_total = train(
        entities, row_acc, relations, src_row, rel_id, dst_owner, dst_row, neg_rows, lengths
    )
    new_rel, new_racc = adagrad(relations, rel_acc, rel_total.astype(F32))
    return (table, accum.reshape(-1), new_rel, new_racc)


def solution(mesh):
    in_specs = (
        P(("grp", "shard"), None),
        P(("grp", "shard")),
        P(),
        P(),
        P(None, "grp", "shard", None),
        P(None, "grp", "shard", None),
        P(None, "grp", "shard", None, None),
        P(None, "grp", "shard", None),
        P(None, "grp", "shard"),
        P(None, "grp", "shard"),
    )
    out_specs = (P(("grp", "shard"), None), P(("grp", "shard")), P(), P())
    return jax.shard_map(
        per_device, mesh=mesh, in_specs=in_specs, out_specs=out_specs, check_vma=False
    )
```

```python
import functools
import jax
import jax.numpy as jnp
from jax import lax
from jax.experimental import pallas as pl
from jax.experimental.pallas import tpu as pltpu
from jax.sharding import PartitionSpec as P

LEARN_RATE = 0.3
MESH = pl.DeviceIdType.MESH
F32 = jnp.float32
BF16 = jnp.bfloat16
LANES = 256


def dot(a, b):
    return jnp.dot(a, b, preferred_element_type=F32)


def hot(index, size):
    places = lax.broadcasted_iota(jnp.int32, (index.shape[0], size), 1)
    return jnp.where(places == index, 1.0, 0.0).astype(BF16)


def hot_t(index, size, first=0):
    places = lax.broadcasted_iota(jnp.int32, (size, index.shape[1]), 0) + first
    return jnp.where(places == index, 1.0, 0.0).astype(BF16)


def train_kernel(groups, shards, edges, capacity, n_own, *refs):
    (entities, row_acc, relations, src_row, rel_id, dst_owner, dst_row, neg_rows, lengths,
     table, acc_out, rel_out, square_out,
     meta, meta_t, requests_2, asked_2, asked_next, asked_t, chunks, high, low, table_bf, acc_t, square_t,
     own_negs, negs_2, sent, queries, got_2, back_2, neg_send, pair_got_2, pair_sum, neg_got_2,
     src_emb, rel_rows_2, query_bf, query_grad, src_grad, rel_grad, neg_acc, total,
     by_slot, by_slot_t, by_asked_t, by_rel_t,
     half, rel_got_c, got_x, got_y, sum_x, sum_y, got_x2, got_y2, last, got_z,
     chunk_sem, req_send, req_recv, neg_sems, row_send, row_recv, pair_sems,
     ngr_send, ngr_recv, grad_send, grad_recv, next_sem, rel_send, rel_recv) = refs

    rows, width = table.shape
    n_rel = relations.shape[0]
    n_neg = shards * n_own
    n_side = n_neg // 2
    depth = shards // 2
    slots = shards * capacity
    g, s = lax.axis_index("grp"), lax.axis_index("shard")
    next_g, prev_g = lax.rem(g + 1, groups), lax.rem(g + groups - 1, groups)
    tile = edges // 3
    chunk = lambda ref, i, size: ref.at[pl.ds(pl.multiple_of(i * size, 16), size)]
    span = lambda ref, at, size: ref.at[pl.ds(pl.multiple_of(at, 16), size)]

    x, y_hi, core = g // 4, lax.rem(g // 2, 2), lax.rem(g, 2)
    z, y_lo = s // 2, lax.rem(s, 2)
    y = y_hi * 2 + y_lo
    pair_s = z * 2 + 1 - y_lo
    along = lambda k: lax.rem(z + k, depth) * 2 + y_lo

    def device(x, y, z, core):
        return (x * 4 + (y // 2) * 2 + core, z * 2 + lax.rem(y, 2))

    x_at = lambda k: lax.rem(x + k, 4)
    y_at = lambda k: lax.rem(y + k, 4)
    z_at = lambda k: lax.rem(z + k, 8)
    x_dev = lambda k: device(x_at(k), y, z, core)
    y_dev = lambda k: device(x, y_at(k), z, core)
    z_dev = lambda k: device(x, y, z_at(k), core)
    core_dev = device(x, y, z, 1 - core)

    def each(begin, end, body):
        def step(k, carry):
            body(k)
            return carry

        lax.fori_loop(begin, end, step, 0)

    barrier = pltpu.get_barrier_semaphore()

    def greet(where):
        pl.semaphore_signal(barrier, inc=1, device_id=where, device_id_type=MESH)

    each(1, shards, lambda k: greet((g, lax.rem(s + shards - k, shards))))
    others = [(prev_g, s), core_dev] + [x_dev(k) for k in (1, 2, 3)] + [y_dev(k) for k in (1, 2, 3)]
    for other in others:
        greet(other)

    rel_steps = n_rel // chunks.shape[1]

    def load(i):
        return pltpu.make_async_copy(
            chunk(relations, i, chunks.shape[1]), chunks.at[i % 2], chunk_sem.at[i % 2]
        )

    load(0).start()
    load(1).start()

    table[...] = entities[...]
    table_bf[...] = entities[...].astype(BF16)
    requests_2[...] = jnp.zeros_like(requests_2)
    for t in range(2):
        requests_2[t, shards, 0:1, :n_own] = neg_rows[t]

    def name_negatives(named):
        column = jnp.transpose(named[shards])[:n_own, 0:1]
        own_negs[...] = dot(hot(column, rows), table_bf[...]).astype(BF16)

    name_negatives(requests_2.at[0])
    def index_edges():
        for t in range(2):
            meta[t : t + 1, :] = dst_owner[t, 0]
            meta[2 + t : 3 + t, :] = src_row[t, 0]
            meta[4 + t : 5 + t, :] = rel_id[t, 0]
        meta[6:8, :] = jnp.zeros((2, edges), jnp.int32)
        meta_t[...] = jnp.transpose(meta[...])

    def plan(t):
        lower_tri = jnp.where(
            lax.broadcasted_iota(jnp.int32, (128, 128), 1)
            < lax.broadcasted_iota(jnp.int32, (128, 128), 0),
            1.0,
            0.0,
        ).astype(BF16)
        shard_rows = lax.broadcasted_iota(jnp.int32, (shards, 128), 0)
        base = jnp.zeros((1, 128), F32)
        upper = jnp.zeros((shards, LANES), F32)
        lower = jnp.zeros((shards, LANES), F32)
        for b in range(edges // 128):
            at = slice(b * 128, b * 128 + 128)
            owner = meta_t[at, t : t + 1]
            chosen = hot(owner, 128)
            chosen_f = chosen.astype(F32)
            count = dot(lower_tri, chosen) + base
            rank = jnp.sum(count * chosen_f, axis=1, keepdims=True).astype(jnp.int32)
            base = base + jnp.sum(chosen_f, axis=0, keepdims=True)
            meta_t[at, 6 + t : 7 + t] = owner * capacity + rank
            by_rank = hot(rank, LANES)
            row = dst_row[t, 0, :, at]
            named = meta[t : t + 1, at] == shard_rows
            part = lambda value: dot(jnp.where(named, value.astype(F32), 0.0).astype(BF16), by_rank)
            upper = upper + part(lax.shift_right_logical(row, 5))
            lower = lower + part(row & 31)
        asking = (upper * 32.0 + lower).astype(jnp.int32)
        for o in range(shards):
            requests_2[t, o, 0:1, :] = asking[o : o + 1, :]

    def request_copy(t, k):
        target = lax.rem(s + k, shards)
        return pltpu.make_async_remote_copy(
            src_ref=requests_2.at[t, target], dst_ref=asked_2.at[t, s],
            send_sem=req_send.at[t, k], recv_sem=req_recv.at[t, k],
            device_id=(g, target), device_id_type=MESH,
        )

    def ask(t):
        each(1, shards, lambda k: request_copy(t, k).start())
        asked_2[t, s] = requests_2[t, s]
        asked_2[t, shards] = requests_2[t, shards]

    index_edges()
    plan(0)
    pl.semaphore_wait(barrier, shards - 1 + len(others))

    forward = pltpu.make_async_remote_copy(
        src_ref=asked_2.at[1], dst_ref=asked_next, send_sem=next_sem.at[0], recv_sem=next_sem.at[1],
        device_id=(next_g, s), device_id_type=MESH,
    )

    def look_relations(t):
        def step(i, carry):
            at = pl.ds(pl.multiple_of(i * tile, 128), tile)
            picked = hot(meta_t[at, :][:, 4 + t : 5 + t], n_rel)
            rel_rows_2[t, at, :] = dot(picked, high[...]) + dot(picked, low[...])
            return carry

        lax.fori_loop(0, 3, step, 0)

    def round_of(t):
        to_g = prev_g if t else g
        from_g = next_g if t else g
        first = 0 if t else 1
        negs, got, back = negs_2.at[t], got_2.at[t], back_2.at[t]
        pair_got, neg_got, rel_rows = pair_got_2.at[t], neg_got_2.at[t], rel_rows_2.at[t]
        wanted = asked_next if t else asked_2.at[0]
        limit = lengths[0:1, t : t + 1]

        def live(i):
            place = lax.broadcasted_iota(jnp.int32, (tile, 1), 0) + i * tile
            return place < limit

        my_block = y_lo * depth + z

        def neg_copy(k):
            return pltpu.make_async_remote_copy(
                src_ref=own_negs, dst_ref=chunk(negs, my_block, n_own),
                send_sem=neg_sems.at[t, 0, k], recv_sem=neg_sems.at[t, 1, k],
                device_id=(to_g, along(k)), device_id_type=MESH,
            )

        neg_pair = pltpu.make_async_remote_copy(
            src_ref=chunk(negs, y_lo, n_side), dst_ref=chunk(negs, y_lo, n_side),
            send_sem=neg_sems.at[t, 0, depth], recv_sem=neg_sems.at[t, 1, depth],
            device_id=(g, pair_s), device_id_type=MESH,
        )

        def row_copy(k):
            target = lax.rem(s + k, shards)
            return pltpu.make_async_remote_copy(
                src_ref=chunk(sent, target, capacity), dst_ref=chunk(got, s, capacity),
                send_sem=row_send.at[t, k], recv_sem=row_recv.at[t, k],
                device_id=(to_g, target), device_id_type=MESH,
            )

        pair_copy = pltpu.make_async_remote_copy(
            src_ref=chunk(neg_send, 1 - y_lo, n_side), dst_ref=pair_got,
            send_sem=pair_sems.at[t, 0], recv_sem=pair_sems.at[t, 1],
            device_id=(g, pair_s), device_id_type=MESH,
        )

        def neg_grad_copy(k):
            return pltpu.make_async_remote_copy(
                src_ref=chunk(pair_sum, z_at(k), n_own), dst_ref=chunk(neg_got, z, n_own),
                send_sem=ngr_send.at[t, k], recv_sem=ngr_recv.at[t, k],
                device_id=(from_g, along(k)), device_id_type=MESH,
            )

        def query_copy(k):
            target = lax.rem(s + k, shards)
            return pltpu.make_async_remote_copy(
                src_ref=chunk(queries, target, capacity), dst_ref=chunk(back, s, capacity),
                send_sem=grad_send.at[t, k], recv_sem=grad_recv.at[t, k],
                device_id=(from_g, target), device_id_type=MESH,
            )

        if t:
            forward.wait()
            name_negatives(asked_next)
        else:
            ask(0)
            negs[pl.ds(pl.multiple_of(my_block * n_own, 16), n_own), :] = own_negs[...]
        each(first, depth, lambda k: neg_copy(k).start())

        if t == 0:
            acc_t[...] = jnp.transpose(row_acc[...])
            for i in range(rel_steps):
                load(i).wait()
                value = chunks[i % 2]
                top = value.astype(BF16)
                at = slice(i * chunks.shape[1], (i + 1) * chunks.shape[1])
                high[at, :] = top
                low[at, :] = (value - top.astype(F32)).astype(BF16)
                if i + 2 < rel_steps:
                    load(i + 2).start()
            each(1, shards, lambda k: request_copy(0, k).wait())

        def answer(who):
            columns = jnp.transpose(wanted[who])[:capacity, :]
            asked_t[pl.ds(pl.multiple_of(who * capacity, 16), capacity), :] = columns
            return dot(hot(columns[:, 0:1], rows), table_bf[...]).astype(BF16)

        def send_rows(k):
            target = lax.rem(s + k, shards)
            sent[pl.ds(pl.multiple_of(target * capacity, 16), capacity), :] = answer(target)
            row_copy(k).start()

        each(first, shards, send_rows)
        if t == 0:
            own_block = pl.ds(pl.multiple_of(s * capacity, 16), capacity)
            sent[own_block, :] = answer(s)
            got[own_block, :] = sent[own_block, :]
        each(first, depth, lambda k: neg_copy(k).wait())
        neg_pair.start()

        if t == 0:
            look_relations(0)

        def look_sources(i, carry):
            at = pl.ds(pl.multiple_of(i * tile, 128), tile)
            emb = dot(hot(meta_t[at, :][:, 2 + t : 3 + t], rows), table_bf[...])
            src_emb[at, :] = emb.astype(BF16)
            query_bf[at, :] = jnp.where(live(i), emb * rel_rows[at, :], 0.0).astype(BF16)
            return carry

        lax.fori_loop(0, 3, look_sources, 0)

        slot_row = jnp.transpose(meta_t[...])[6 + t : 7 + t, :]

        def mark_slots_t(i):
            at = pl.multiple_of(i * 128, 128)
            by_slot_t[pl.ds(at, 128), :] = hot_t(slot_row, 128, at)

        def query_block(target):
            at = pl.ds(pl.multiple_of(target * capacity, 16), capacity)
            return dot(by_slot_t[at, :], query_bf[...]).astype(BF16)

        def send_query(k):
            target = lax.rem(s + k, shards)
            queries[pl.ds(pl.multiple_of(target * capacity, 16), capacity), :] = query_block(target)
            if t:
                row_copy(k).wait_send()
            query_copy(k).start()

        def send_queries():
            each(0, slots // 128, mark_slots_t)
            each(first, shards, send_query)
            if t == 0:
                back[own_block, :] = query_block(s)

        if t == 0:
            send_queries()
        neg_pair.wait()
        neg_acc[...] = jnp.zeros_like(neg_acc)

        def against_negatives(i, carry):
            at = pl.ds(pl.multiple_of(i * tile, 128), tile)
            query = query_bf[at, :]
            scores = lax.dot_general(
                query, negs[...], (((1,), (1,)), ((), ())), preferred_element_type=F32
            )
            weight = jnp.where(
                live(i), (jnp.tanh(scores * 0.5) + 1.0) * (0.5 / n_neg), 0.0
            ).astype(BF16)
            query_grad[at, :] = dot(weight, negs[...])
            neg_acc[...] += dot(jnp.transpose(query.astype(F32)).astype(BF16), weight)
            return carry

        lax.fori_loop(0, 3, against_negatives, 0)
        neg_send[...] = jnp.transpose(neg_acc[...]).astype(BF16)
        pair_copy.start()

        def mark_slots(i):
            at = pl.ds(pl.multiple_of(i * 128, 128), 128)
            by_slot[at, :] = hot(meta_t[at, :][:, 6 + t : 7 + t], slots)

        each(0, edges // 128, mark_slots)

        asked_rows = jnp.transpose(asked_t[...])[0:1, :]

        def mark_asked(i):
            at = pl.multiple_of(i * 128, 128)
            by_asked_t[pl.ds(at, 128), :] = hot_t(asked_rows, 128, at)

        each(0, rows // 128, mark_asked)

        n_half, n_quarter = n_rel // 2, n_rel // 4
        mine, theirs = core * n_half, (1 - core) * n_half
        if t:

            def mark_relations(i):
                at = pl.multiple_of(i * 128, 128)
                by_rel_t[pl.ds(at, 128), :] = hot_t(meta[4 + t : 5 + t, :], 128, theirs + at)

            each(0, n_half // 128, mark_relations)

        if t:
            send_queries()
        pair_copy.wait()
        mine_side = pl.ds(pl.multiple_of(y_lo * n_side, 16), n_side)
        pair_sum[...] = (neg_send[mine_side, :].astype(F32) + pair_got[...].astype(F32)).astype(BF16)
        if t == 0:
            own = pl.ds(pl.multiple_of(z * n_own, 16), n_own)
            neg_got[own, :] = pair_sum[own, :]
        if t == 0:
            each(1, depth, lambda k: neg_grad_copy(k).start())
        if t == 0:
            plan(1)
            ask(1)

        if t == 0:
            each(1, shards, lambda k: row_copy(k).wait_send())
        each(first, shards, lambda k: row_copy(k).wait_recv())

        def send_held():
            each(0, depth, lambda k: neg_grad_copy(k).start())

        def positives(i, carry):
            at = pl.ds(pl.multiple_of(i * tile, 128), tile)
            emb = src_emb[at, :].astype(F32)
            rel = rel_rows[at, :]
            query = emb * rel
            dst = dot(by_slot[at, :], got[...])
            positive = jnp.sum(query * dst, axis=1, keepdims=True)
            weight = jnp.where(live(i), (jnp.tanh(positive * -0.5) + 1.0) * -0.5, 0.0)
            grad = weight * dst + query_grad[at, :]
            src_grad[at, :] = (grad * rel).astype(BF16)
            rel_grad[at, :] = (grad * emb).astype(BF16)
            return carry

        lax.fori_loop(0, 3, positives, 0)

        def scatter_sources():
            def step(i):
                at = pl.multiple_of(i * 256, 256)
                total[pl.ds(at, 256), :] = dot(hot_t(meta[2 + t : 3 + t, :], 256, at), src_grad[...])

            each(0, rows // 256, step)

        def take_queries():
            each(first, shards, lambda k: query_copy(k).wait())

            def weigh(i):
                at = pl.ds(pl.multiple_of(i * 384, 128), 384)
                query = back[at, :].astype(F32)
                positive = jnp.sum(query * sent[at, :].astype(F32), axis=1, keepdims=True)
                weight = (jnp.tanh(positive * -0.5) + 1.0) * -0.5
                back[at, :] = (weight * query).astype(BF16)

            each(0, slots // 384, weigh)

            def add(i):
                at = pl.ds(pl.multiple_of(i * 256, 256), 256)
                total[at, :] += dot(by_asked_t[at, :], back[...])

            each(0, rows // 256, add)

        def take_negatives():
            each(first, depth, lambda k: neg_grad_copy(k).wait())
            summed = neg_got[0:n_own, :].astype(F32)
            for k in range(1, depth):
                summed += neg_got[k * n_own : (k + 1) * n_own, :].astype(F32)
            upper = summed.astype(BF16)
            lower = (summed - upper.astype(F32)).astype(BF16)
            named = wanted[shards][0:1, :n_own]
            for i in range(rows // 128):
                at = slice(i * 128, i * 128 + 128)
                picked = hot_t(named, 128, i * 128)
                grad = total[at, :] + dot(picked, upper) + dot(picked, lower)
                acc = acc_t[:, i : i + 1] + jnp.sum(grad * grad, axis=1, keepdims=True) * (1.0 / width)
                fresh = table[at, :] - LEARN_RATE * grad / jnp.sqrt(acc)
                acc_t[:, i : i + 1] = acc
                table[at, :] = fresh
                if t == 0:
                    table_bf[at, :] = fresh.astype(BF16)

        if t == 0:
            scatter_sources()

            def scatter(i):
                at = pl.multiple_of(i * 512, 512)
                part = dot(hot_t(meta[4:5, :], 512, at), rel_grad[...])
                half[pl.ds(at, 512), :] = part.astype(BF16)

            each(0, n_rel // 512, scatter)
            look_relations(1)
            each(1, shards, lambda k: request_copy(1, k).wait())
            forward.start()
            take_queries()
            take_negatives()
            return

        big, small, least = n_quarter // 4, n_quarter // 16, n_rel // 256

        def rel_copy(src, dst, sem, where):
            return pltpu.make_async_remote_copy(
                src_ref=src, dst_ref=dst, send_sem=rel_send.at[sem], recv_sem=rel_recv.at[sem],
                device_id=where, device_id_type=MESH,
            )

        def run(copies):
            for copy in copies:
                copy.start()
            return copies

        def finish(copies):
            for copy in copies:
                copy.wait()

        def scatter_theirs(i):
            at = pl.multiple_of(i * 512, 512)
            where = pl.ds(pl.multiple_of(theirs + at, 512), 512)
            part = dot(by_rel_t[pl.ds(at, 512), :], rel_grad[...])
            half[where, :] = (half[where, :].astype(F32) + part).astype(BF16)

        def scatter_mine(i):
            at = pl.multiple_of(mine + i * 512, 512)
            part = dot(hot_t(meta[5:6, :], 512, at), rel_grad[...])
            half[pl.ds(at, 512), :] = (half[pl.ds(at, 512), :].astype(F32) + part).astype(BF16)

        copies = []
        for i in range(2):
            each(i * (n_half // 1024), (i + 1) * (n_half // 1024), scatter_theirs)
            copies += run(
                [
                    rel_copy(
                        span(half, theirs + i * n_quarter, n_quarter),
                        span(rel_got_c, i * n_quarter, n_quarter), 40 * i, core_dev,
                    )
                ]
            )
        each(0, n_half // 512, scatter_mine)
        finish(copies)

        def add_core(i):
            at = pl.multiple_of(i * 256, 256)
            mine_at = pl.ds(pl.multiple_of(mine + at, 256), 256)
            value = half[mine_at, :].astype(F32) + rel_got_c[pl.ds(at, 256), :].astype(F32)
            rel_got_c[pl.ds(at, 256), :] = value.astype(BF16)

        each(0, n_half // 256, add_core)
        chip = rel_got_c
        copies = run(
            [rel_copy(span(chip, x_at(k) * big, big), got_x.at[k - 1], k, x_dev(k)) for k in (1, 2, 3)]
            + [
                rel_copy(span(chip, n_quarter + y_at(k) * big, big), got_y.at[k - 1], 3 + k, y_dev(k))
                for k in (1, 2, 3)
            ]
        )
        scatter_sources()
        finish(copies)

        def sum_of(ref, at, size, arrived):
            value = ref[pl.ds(pl.multiple_of(at, 16), size), :].astype(F32)
            for k in range(arrived.shape[0]):
                value += arrived[k].astype(F32)
            return value.astype(BF16)

        sum_x[...] = sum_of(chip, x * big, big, got_x)
        sum_y[...] = sum_of(chip, n_quarter + y * big, big, got_y)
        copies = run(
            [rel_copy(span(sum_x, y_at(k) * small, small), got_y2.at[k - 1], 6 + k, y_dev(k)) for k in (1, 2, 3)]
            + [rel_copy(span(sum_y, x_at(k) * small, small), got_x2.at[k - 1], 9 + k, x_dev(k)) for k in (1, 2, 3)]
        )
        finish(copies)
        last[0:small, :] = sum_of(sum_x, y * small, small, got_y2)
        last[small : 2 * small, :] = sum_of(sum_y, x * small, small, got_x2)
        copies = run(
            [rel_copy(span(last, z_at(k) * least, least), got_z.at[k - 1], 12 + k, z_dev(k)) for k in range(1, 8)]
        )
        finish(copies)
        side = z // 4
        at_x = mine + x * big + y * small
        at_y = mine + n_quarter + y * big + x * small
        at_z = at_x + side * (at_y - at_x) + lax.rem(z, 4) * least
        rel_out[pl.ds(pl.multiple_of(at_z, 16), least), :] = sum_of(last, z * least, least, got_z)
        same = lambda at, size: [span(rel_out, at, size)] * 2
        finish(run([rel_copy(*same(at_z, least), 19 + k, z_dev(k)) for k in range(1, 8)]))
        copies = run(
            [rel_copy(*same(at_x, small), 26 + k, y_dev(k)) for k in (1, 2, 3)]
            + [rel_copy(*same(at_y, small), 29 + k, x_dev(k)) for k in (1, 2, 3)]
        )
        send_held()
        finish(copies)
        copies = run(
            [rel_copy(*same(mine + x * big, big), 32 + k, x_dev(k)) for k in (1, 2, 3)]
            + [rel_copy(*same(mine + n_quarter + y * big, big), 35 + k, y_dev(k)) for k in (1, 2, 3)]
        )
        take_queries()
        finish(copies)
        copies = run([rel_copy(*same(mine, n_half), 39, core_dev)])
        take_negatives()

        def square(begin):
            for i in range(n_half // 128):
                at = pl.ds(pl.multiple_of(begin + i * 128, 128), 128)
                value = rel_out[at, :].astype(F32)
                square_t[:, part_of + i : part_of + i + 1] = jnp.sum(
                    value * value, axis=1, keepdims=True
                )

        part_of = 0
        square(mine)
        finish(copies)
        part_of = n_half // 128
        square(theirs)
        squares = jnp.transpose(square_t[...])
        part_of = n_half // 128
        square_out[pl.ds(pl.multiple_of(core * part_of, 8), part_of), :] = squares[:part_of, :]
        square_out[pl.ds(pl.multiple_of((1 - core) * part_of, 8), part_of), :] = squares[part_of:, :]

    round_of(0)
    round_of(1)
    acc_out[...] = jnp.transpose(acc_t[...])


def train(entities, row_acc, relations, src_row, rel_id, dst_owner, dst_row, neg_rows, lengths):
    groups, shards = lax.axis_size("grp"), lax.axis_size("shard")
    rows, width = entities.shape
    n_rel, edges, n_own = relations.shape[0], src_row.shape[-1], neg_rows.shape[-1]
    capacity = 2 * edges // shards
    n_neg, slots, depth = shards * n_own, shards * capacity, shards // 2
    bf = lambda *shape: pltpu.VMEM(shape + (width,), BF16)
    f32 = lambda *shape: pltpu.VMEM(shape + (width,), F32)
    i32 = lambda *shape: pltpu.VMEM(shape, jnp.int32)
    sems = lambda *shape: pltpu.SemaphoreType.DMA(shape)
    scratch = [
        i32(8, edges), i32(edges, 8),
        i32(2, shards + 1, 8, LANES), i32(2, shards + 1, 8, LANES), i32(shards + 1, 8, LANES), i32(slots, 8),
        f32(2, 512), bf(n_rel), bf(n_rel), bf(rows), pltpu.VMEM((rows // 8, 8), F32),
        pltpu.VMEM((128, n_rel // 128), F32),
        bf(n_own), bf(2, n_neg), bf(slots), bf(slots), bf(2, slots), bf(2, slots),
        bf(n_neg), bf(2, n_neg // 2), bf(n_neg // 2), bf(2, n_neg // 2),
        bf(edges), f32(2, edges), bf(edges), f32(edges), bf(edges), bf(edges),
        pltpu.VMEM((width, n_neg), F32), f32(rows),
        pltpu.VMEM((edges, slots), BF16), pltpu.VMEM((slots, edges), BF16),
        pltpu.VMEM((rows, slots), BF16), pltpu.VMEM((n_rel // 2, edges), BF16),
        bf(n_rel), bf(n_rel // 2),
        bf(3, n_rel // 16), bf(3, n_rel // 16), bf(n_rel // 16), bf(n_rel // 16),
        bf(3, n_rel // 64), bf(3, n_rel // 64), bf(n_rel // 32), bf(7, n_rel // 256),
        sems(2), sems(2, shards), sems(2, shards), sems(2, 2, depth + 1),
        sems(2, shards), sems(2, shards), sems(2, 2),
        sems(2, depth), sems(2, depth), sems(2, shards), sems(2, shards),
        sems(2), sems(41), sems(41),
    ]
    vmem = pl.BlockSpec(memory_space=pltpu.VMEM)
    return pl.pallas_call(
        functools.partial(train_kernel, groups, shards, edges, capacity, n_own),
        out_shape=[
            jax.ShapeDtypeStruct((rows, width), F32),
            jax.ShapeDtypeStruct((8, rows // 8), F32),
            jax.ShapeDtypeStruct((n_rel, width), BF16),
            jax.ShapeDtypeStruct((n_rel // 128, 128), F32),
        ],
        in_specs=[vmem, vmem, pl.BlockSpec(memory_space=pl.ANY)] + [vmem] * 6,
        out_specs=[vmem] * 4,
        scratch_shapes=scratch,
        compiler_params=pltpu.CompilerParams(
            collective_id=0, has_side_effects=True, vmem_limit_bytes=56 << 20
        ),
        name="train",
    )(
        entities, row_acc.reshape(8, rows // 8), relations, src_row, rel_id,
        dst_owner[..., 0], dst_row, neg_rows, lengths.reshape(1, 2),
    )


def per_device(
    entities, row_acc, relations, rel_acc, src_row, rel_id, dst_owner, dst_row, neg_rows, lengths
):
    table, accum, rel_total, square = train(
        entities, row_acc, relations, src_row, rel_id, dst_owner, dst_row, neg_rows, lengths
    )
    new_racc = rel_acc + square.reshape(-1) * (1.0 / relations.shape[1])
    new_rel = relations - LEARN_RATE * rel_total.astype(F32) / jnp.sqrt(new_racc)[:, None]
    return (table, accum.reshape(-1), new_rel, new_racc)


def solution(mesh):
    in_specs = (
        P(("grp", "shard"), None),
        P(("grp", "shard")),
        P(),
        P(),
        P(None, "grp", "shard", None),
        P(None, "grp", "shard", None),
        P(None, "grp", "shard", None, None),
        P(None, "grp", "shard", None),
        P(None, "grp", "shard"),
        P(None, "grp", "shard"),
    )
    out_specs = (P(("grp", "shard"), None), P(("grp", "shard")), P(), P())
    return jax.shard_map(
        per_device, mesh=mesh, in_specs=in_specs, out_specs=out_specs, check_vma=False
    )
```
